32 devices in a mesh: space: 8 (over z, x), kern: 4 (over y, core).
Axes of the slice: x: 2, y: 2, z: 4, core: 2. Of those that a mesh axis runs over, the one named last changes fastest.
Arguments:
- mask: bfloat16 [4096, 4096], P('space'), may hold values from -1 to 1
- kernels: float32 [2, 16, 512, 512], P(None, 'kern', 'space'), may hold values from -4 to 4
- target: int32 [1024, 1024], P('space'), may hold values 0 or 1
Outputs:
- gradient: float32 [4096, 4096], P('space')
- resist: float32 [1024, 1024], P('space')
The draws below stay inside these ranges and needn't reach their ends.
All inputs are finite; a program needn't handle non-finite values. No bound on the sum of `target` on one device may be relied on, other than what follows from the above.
Results may differ from the reference program's by a relative error of at most 0.0003.
Values sent between devices are 32-bit elements; how exact they have to be, the bound alone decides.
A program may use at most 64 MiB of HBM per device.

```python
import jax
import jax.numpy as jnp
from jax import lax

N = 4096
B = 512
G = 1024
K = 16


def plant(result, key, least, top_value):
    spot = [jax.random.randint(jax.random.fold_in(key, axis), (), 0, length) for axis, length in enumerate(result.shape)]
    longest = result.shape.index(max(result.shape))
    beside = spot[:longest] + [(spot[longest] + 1) % result.shape[longest]] + spot[longest + 1:]
    return result.at[tuple(spot)].set(least).at[tuple(beside)].set(top_value)


def levels(stream_key, extent, pieces, smallest, high):
    loudness, own = 1.0, jax.random.fold_in(stream_key, 6)
    for dim, shards_of in pieces:
        draws = jnp.exp(jax.random.uniform(jax.random.fold_in(own, dim), (shards_of,), jnp.float32, smallest / len(pieces), high / len(pieces)))
        loudness = loudness * jnp.repeat(draws, extent[dim] // shards_of).reshape([-1 if axis == dim else 1 for axis in range(len(extent))])
    return loudness


def scatter_about(stream_key, extent, scale, most, pieces=(), kind=jnp.bfloat16):
    loudness = levels(stream_key, extent, pieces, -0.22, 0.18) if pieces else 1.0
    result = jax.random.normal(stream_key, extent, jnp.float32) * scale * loudness
    return jnp.minimum(jnp.maximum(result, -most), most).astype(kind)


def setup_inputs(seed: int = 0) -> dict:
    keys = jax.random.split(jax.random.key(seed), 4)
    return {
        "mask": jnp.clip(jax.random.uniform(keys[0], (N, N), jnp.float32, -1.0, 1.0) * levels(keys[0], (N, N), ((0, 8),), -0.4, 0.0), -1.0, 1.0).astype(jnp.bfloat16),
        "kernels": scatter_about(keys[1], (2, K, B, B), 0.3, 4.0, ((1, 4), (2, 8)), jnp.float32),
        "target": plant((jax.random.randint(keys[2], (G, G), 0, 2) < 1).astype(jnp.int32), jax.random.fold_in(keys[2], 1), 0, 1),
    }


steepness = 8.0
threshold = 1.5
highest = lax.Precision.HIGHEST


def phases(left, right, modulus):
    product = (left[:, None] * right[None, :]) % modulus
    return product.astype(jnp.float32) * (2.0 * jnp.pi / modulus)


def column_table(pixels, frequency, length):
    angle = phases(pixels, frequency, length)
    return jnp.concatenate([jnp.cos(angle), -jnp.sin(angle)], axis=1)


def row_table(pixels, frequency, length):
    angle = phases(pixels, frequency, length)
    return jnp.concatenate([jnp.cos(angle), -jnp.sin(angle)], axis=1) / length


def grid_table(frequency, points):
    angle = phases(frequency, jnp.arange(points, dtype=jnp.int32), points)
    return jnp.concatenate([jnp.cos(angle), jnp.sin(angle)], axis=1)


def reference(mask, kernels, target):
    frequency = jnp.arange(B, dtype=jnp.int32) - B // 2
    pixels = jnp.arange(N, dtype=jnp.int32)
    col_tab = column_table(pixels, frequency, N)
    row_tab = row_table(pixels, frequency, N)
    grid = grid_table(frequency, G)
    columns = lax.dot_general(col_tab, mask.astype(jnp.float32), (((0,), (1,)), ((), ())), precision=highest)
    total = jnp.dot(columns, row_tab, precision=highest)
    spec_re = total[:B, :B] - total[B:, B:]
    spec_im = total[:B, B:] + total[B:, :B]
    kern_re = kernels[0]
    kern_im = kernels[1]
    prod_re = kern_re * spec_re - kern_im * spec_im
    prod_im = kern_re * spec_im + kern_im * spec_re
    lifted = jnp.dot(jnp.stack([prod_re, prod_im]).reshape(2 * K * B, B), grid, precision=highest).reshape(2, K, B, 2 * G)
    coarse_re = lifted[0, :, :, :G] - lifted[1, :, :, G:]
    coarse_im = lifted[0, :, :, G:] + lifted[1, :, :, :G]
    image = lax.dot_general(jnp.stack([coarse_re, coarse_im]), grid, (((2,), (0,)), ((), ())), precision=highest)
    field_re = image[0, :, :, :G] - image[1, :, :, G:]
    field_im = image[0, :, :, G:] + image[1, :, :, :G]
    intensity = jnp.sum(field_re * field_re + field_im * field_im, axis=0) / (B * B)
    resist = jax.nn.sigmoid(steepness * (intensity - threshold))
    slope = 2.0 * (resist - target.astype(jnp.float32)) * steepness * resist * (1.0 - resist)
    scale = 2.0 * slope / (B * B)
    grad_re = scale * field_re
    grad_im = scale * field_im
    mixed = jnp.stack([jnp.concatenate([grad_re, grad_im], axis=-1), jnp.concatenate([grad_im, -grad_re], axis=-1)])
    back = lax.dot_general(grid, mixed, (((1,), (3,)), ((), ())), precision=highest)
    back_re = back[:, 0]
    back_im = back[:, 1]
    mixed_two = jnp.stack([jnp.concatenate([back_re, back_im], axis=-1), jnp.concatenate([back_im, -back_re], axis=-1)])
    spectral = lax.dot_general(mixed_two, grid, (((3,), (1,)), ((), ())), precision=highest)
    kern_swap = jnp.swapaxes(kernels, 1, 2)
    sum_re = jnp.sum(kern_swap[0] * spectral[0] + kern_swap[1] * spectral[1], axis=1)
    sum_im = jnp.sum(kern_swap[0] * spectral[1] - kern_swap[1] * spectral[0], axis=1)
    stacked = jnp.concatenate([jnp.concatenate([sum_re, sum_im], axis=1), jnp.concatenate([sum_im, -sum_re], axis=1)], axis=0)
    delta = lax.dot_general(stacked, row_tab, (((1,), (1,)), ((), ())), precision=highest)
    gradient = lax.dot_general(delta, col_tab, (((0,), (1,)), ((), ())), precision=highest)
    return gradient, resist
```

```python
import functools

import jax
import jax.numpy as jnp
import ml_dtypes
import numpy as np
from jax import lax
from jax.experimental import pallas as pl
from jax.experimental.pallas import tpu as pltpu
from jax.sharding import PartitionSpec as P

N = 4096
B = 512
G = 1024


steepness = 8.0
threshold = 1.5
highest = lax.Precision.HIGHEST
block_limit = 1024


def phases(left, right, modulus):
    product = left[:, None] * right[None, :] % modulus
    return product.astype(jnp.float32) * (2.0 * jnp.pi / modulus)


def column_table(pixels, frequency, length):
    angle = phases(pixels, frequency, length)
    return jnp.concatenate([jnp.cos(angle), -jnp.sin(angle)], axis=1)


def row_table(pixels, frequency, length):
    angle = phases(pixels, frequency, length)
    return jnp.concatenate([jnp.cos(angle), -jnp.sin(angle)], axis=1) / length


def grid_table(frequency, points):
    angle = phases(frequency, jnp.arange(points, dtype=jnp.int32), points)
    return jnp.concatenate([jnp.cos(angle), jnp.sin(angle)], axis=1)


def forward_columns(mask, frequency):
    rows = mask.shape[0]
    span = min(block_limit, N)
    count = frequency.shape[0]

    def step(index, running):
        start = index * span
        table = column_table(start + jnp.arange(span, dtype=jnp.int32), frequency, N)
        piece = lax.dynamic_slice_in_dim(mask, start, span, 1).astype(jnp.float32)
        return running + lax.dot_general(table, piece, (((0,), (1,)), ((), ())), precision=highest)

    running = lax.fori_loop(0, N // span, step, jnp.zeros((2 * count, rows), jnp.float32))
    return running.reshape(2, count, rows)


def forward_rows(arrived):
    count = arrived.shape[1]
    flat = arrived.reshape(2 * count, N)
    frequency = jnp.arange(B, dtype=jnp.int32) - B // 2
    span = min(block_limit, N)

    def step(index, running):
        start = index * span
        table = row_table(start + jnp.arange(span, dtype=jnp.int32), frequency, N)
        piece = lax.dynamic_slice_in_dim(flat, start, span, 1)
        return running + jnp.dot(piece, table, precision=highest)

    running = lax.fori_loop(0, N // span, step, jnp.zeros((2 * count, 2 * B), jnp.float32))
    real_part = running[:count, :B] - running[count:, B:]
    imag_part = running[:count, B:] + running[count:, :B]
    return jnp.stack([real_part, imag_part])


def adjoint_rows(sum_re, sum_im):
    count = sum_re.shape[0]
    stacked = jnp.concatenate(
        [jnp.concatenate([sum_re, sum_im], axis=1), jnp.concatenate([sum_im, -sum_re], axis=1)],
        axis=0,
    )
    frequency = jnp.arange(B, dtype=jnp.int32) - B // 2
    span = min(block_limit, N)

    def step(index, output):
        start = index * span
        table = row_table(start + jnp.arange(span, dtype=jnp.int32), frequency, N)
        piece = lax.dot_general(stacked, table, (((1,), (1,)), ((), ())), precision=highest)
        return lax.dynamic_update_slice_in_dim(output, piece, start, 1)

    output = lax.fori_loop(0, N // span, step, jnp.zeros((2 * count, N), jnp.float32))
    return output.reshape(2, count, N)


def add_columns(total, spectrum, frequency):
    span = min(block_limit, N)

    def step(index, running):
        start = index * span
        table = column_table(start + jnp.arange(span, dtype=jnp.int32), frequency, N)
        piece = lax.dot_general(spectrum, table, (((0,), (1,)), ((), ())), precision=highest)
        current = lax.dynamic_slice_in_dim(running, start, span, 1)
        return lax.dynamic_update_slice_in_dim(running, current + piece, start, 1)

    return lax.fori_loop(0, N // span, step, total)


def local(mask, kernels, target):
    rows = mask.shape[0]
    kern_count = lax.axis_size("kern")
    space_count = lax.axis_size("space")
    group = lax.axis_index("kern")
    per_space = B // space_count
    per_group = per_space // kern_count
    frequency = jnp.arange(B, dtype=jnp.int32) - B // 2
    subset = (
        per_space * jnp.arange(space_count, dtype=jnp.int32)[:, None]
        + per_group * group
        + jnp.arange(per_group, dtype=jnp.int32)[None, :]
    )
    columns = forward_columns(mask, subset.reshape(-1) - B // 2)
    arrived = lax.all_to_all(columns, "space", split_axis=1, concat_axis=2, tiled=True)
    spectrum = lax.all_gather(forward_rows(arrived), "kern", axis=1, tiled=True)
    kern_swap = jnp.swapaxes(kernels, 1, 2)
    kernel_count = kern_swap.shape[2]
    spec_re = spectrum[0][:, None, :]
    spec_im = spectrum[1][:, None, :]
    prod_re = kern_swap[0] * spec_re - kern_swap[1] * spec_im
    prod_im = kern_swap[0] * spec_im + kern_swap[1] * spec_re
    grid = grid_table(frequency, G)
    lifted = jnp.dot(
        jnp.stack([prod_re, prod_im]).reshape(2 * per_space * kernel_count, B),
        grid,
        precision=highest,
    )
    lifted = lifted.reshape(2, per_space, kernel_count, 2 * G)
    coarse_re = lifted[0, :, :, :G] - lifted[1, :, :, G:]
    coarse_im = lifted[0, :, :, G:] + lifted[1, :, :, :G]
    coarse = jnp.stack([coarse_re, coarse_im], axis=1)
    gathered = lax.all_to_all(coarse, "space", split_axis=3, concat_axis=0, tiled=True)
    grid_rows = gathered.shape[3]
    image = lax.dot_general(
        gathered.reshape(B, 2 * kernel_count * grid_rows),
        grid,
        (((0,), (0,)), ((), ())),
        precision=highest,
    )
    image = image.reshape(2, kernel_count, grid_rows, 2 * G)
    field_re = image[0, :, :, :G] - image[1, :, :, G:]
    field_im = image[0, :, :, G:] + image[1, :, :, :G]
    partial_light = jnp.sum(field_re * field_re + field_im * field_im, axis=0) / (B * B)
    intensity = lax.psum(partial_light, "kern")
    resist = jax.nn.sigmoid(steepness * (intensity - threshold))
    slope = 2.0 * (resist - target.astype(jnp.float32)) * steepness * resist * (1.0 - resist)
    scale = 2.0 * slope / (B * B)
    grad_re = scale * field_re
    grad_im = scale * field_im
    mixed = jnp.stack(
        [
            jnp.concatenate([grad_re, grad_im], axis=-1),
            jnp.concatenate([grad_im, -grad_re], axis=-1),
        ]
    )
    mixed = mixed.reshape(2 * kernel_count * grid_rows, 2 * G)
    backward = lax.dot_general(grid, mixed, (((1,), (1,)), ((), ())), precision=highest)
    backward = backward.reshape(B, 2, kernel_count, grid_rows)
    returned = lax.all_to_all(backward, "space", split_axis=0, concat_axis=3, tiled=True)
    back_re = returned[:, 0]
    back_im = returned[:, 1]
    mixed_two = jnp.stack(
        [
            jnp.concatenate([back_re, back_im], axis=-1),
            jnp.concatenate([back_im, -back_re], axis=-1),
        ]
    )
    mixed_two = mixed_two.reshape(2 * per_space * kernel_count, 2 * G)
    spectral = lax.dot_general(mixed_two, grid, (((1,), (1,)), ((), ())), precision=highest)
    spectral = spectral.reshape(2, per_space, kernel_count, B)
    sum_re = jnp.sum(kern_swap[0] * spectral[0] + kern_swap[1] * spectral[1], axis=1)
    sum_im = jnp.sum(kern_swap[0] * spectral[1] - kern_swap[1] * spectral[0], axis=1)
    empty = jnp.zeros((rows, N), jnp.float32)
    shares = (
        lax.psum_scatter(sum_re, "kern", scatter_dimension=0, tiled=True),
        lax.psum_scatter(sum_im, "kern", scatter_dimension=0, tiled=True),
    )
    delta = adjoint_rows(shares[0], shares[1])
    landed = lax.all_to_all(delta, "space", split_axis=2, concat_axis=1, tiled=True)
    ordering = (
        per_group * jnp.arange(kern_count, dtype=jnp.int32)[:, None, None]
        + per_space * jnp.arange(space_count, dtype=jnp.int32)[None, :, None]
        + jnp.arange(per_group, dtype=jnp.int32)[None, None, :]
    )
    ordered_freq = ordering.reshape(-1) - B // 2
    piece = lax.all_gather(landed, "kern", axis=1, tiled=True)
    width = piece.shape[1]
    gradient = add_columns(empty, piece.reshape(2 * width, rows), ordered_freq)
    return (gradient, resist)


MESH = pl.DeviceIdType.MESH


def split_constant(values):
    high = values.astype(np.float32).astype(ml_dtypes.bfloat16)
    low = (values - high.astype(np.float64)).astype(ml_dtypes.bfloat16)
    return jnp.asarray(high), jnp.asarray(low)


def pixel_table():
    f = np.arange(B) - B // 2
    angle = (f[:, None] * np.arange(N)) % N * (2 * np.pi / N)
    return jnp.asarray(np.concatenate([np.cos(angle), -np.sin(angle)]).astype(np.float32))


def coarse_tables():
    f = np.arange(B) - B // 2
    points = np.arange(G)
    angle = (f[:, None] * points[None, :]) % G * (2 * np.pi / G)
    c, s = np.cos(angle), np.sin(angle)
    order = np.arange(G).reshape(8, 2, 2, G // 32).transpose(1, 2, 0, 3).reshape(2, G // 2)
    lift = np.stack([np.block([[c.T[o], -s.T[o]], [s.T[o], c.T[o]]]) for o in order])
    W = G // PARTS
    image = np.stack([np.concatenate([c[:, j * W : j * W + W], s[:, j * W : j * W + W]], 1) for j in range(PARTS)])
    return split_constant(lift) + split_constant(image)


def halves(value):
    high = value.astype(jnp.bfloat16)
    return high, (value - high.astype(jnp.float32)).astype(jnp.bfloat16)


def dot3(ah, al, bh, bl, dims):
    d = functools.partial(lax.dot_general, dimension_numbers=(dims, ((), ())), preferred_element_type=jnp.float32)
    return d(ah, bh) + (d(al, bh) + d(ah, bl))


NN = ((1,), (0,))
NT = ((1,), (1,))
PARTS = 4
DIMS = "yhlx"
ORDERS = ("xylh", "ylxh", "lxyh", "yxlh")
SPACE_ORDERS = ("xlh", "lxh", "xlh", "lxh")


def remote(src, dst, send, recv, device):
    return pltpu.make_async_remote_copy(
        src_ref=src, dst_ref=dst, send_sem=send, recv_sem=recv, device_id=device, device_id_type=MESH
    )


def crossed(v):
    return 2 * lax.rem(v, 2) + v // 2


def index(dims, fixed, lanes):
    return tuple(fixed.get(d, slice(None)) for d in dims) + (slice(None), lanes)


def without(dims, gone):
    return "".join(d for d in dims if d not in gone)


class Scatter:
    def __init__(self, me, partner, src, bufs, dims, order, lanes, send, recv):
        self.me, self.partner, self.refs, self.dims = me, partner, [src] + list(bufs), dims
        self.order, self.lanes, self.send, self.recv = order, lanes, send, recv

    def copy(self, t):
        d = self.order[t]
        left = without(self.dims, self.order[:t])
        return remote(
            self.refs[t].at[index(left, {d: 1 - self.me[d]}, self.lanes)],
            self.refs[t + 1].at[index(without(left, d), {}, self.lanes)],
            self.send.at[t], self.recv.at[t], self.partner[d],
        )

    def start(self, t):
        self.copy(t).start()

    def finish(self, t):
        self.copy(t).wait_recv()
        d = self.order[t]
        left = without(self.dims, self.order[:t])
        own = self.refs[t][index(left, {d: self.me[d]}, self.lanes)]
        there = index(without(left, d), {}, self.lanes)
        self.refs[t + 1][there] = self.refs[t + 1][there] + own

    def drain(self):
        for t in range(len(self.order)):
            self.copy(t).wait_send()


class Gather:
    def __init__(self, me, partner, ref, dims, order, lanes, send, recv):
        self.me, self.partner, self.ref, self.dims = me, partner, ref, dims
        self.order, self.lanes, self.send, self.recv = order, lanes, send, recv

    def copy(self, t, theirs):
        fixed = {d: self.me[d] for d in self.order[t:]}
        if theirs:
            fixed[self.order[t]] = 1 - fixed[self.order[t]]
        view = self.ref.at[index(self.dims, fixed, self.lanes)]
        return remote(view, view, self.send.at[t], self.recv.at[t], self.partner[self.order[t]])

    def start(self, t):
        self.copy(t, False).start()

    def finish(self, t):
        self.copy(t, True).wait_recv()

    def drain(self):
        for t in range(len(self.order)):
            self.copy(t, False).wait_send()


def imaging_kernel(
    part_ref, kern_mine, target_ref, lh_hbm, ll_hbm, th_hbm, tl_hbm,
    out_ref, resist_ref,
    lh, ll, th, tl, table_sem,
    kbuf, p0, p1, p2, spec, ph, pw, cout, cin, ch, cl, field,
    light, l0, l1, l2, l3, slope, grad, gin, acc, sums, s0, s1, s2, s3,
    ks, kr_, ps, pr_, as_, ar, xs, xr, ls, lr, gs, gr, cs, cr, ss, sr_, os_, or_, fs, fr, us, ur,
):
    H, W, C = G // 2, G // PARTS, B // 2
    sp, kq = lax.axis_index("space"), lax.axis_index("kern")
    z, x = sp // 2, lax.rem(sp, 2)
    y, core = kq // 2, lax.rem(kq, 2)
    me = {"y": y, "h": z // 2, "l": lax.rem(z, 2), "x": x}
    partner = {
        "y": (sp, (1 - y) * 2 + core),
        "x": (z * 2 + 1 - x, kq),
        "l": ((z + 1 - 2 * me["l"]) * 2 + x, kq),
        "h": (lax.rem(z + 2, 4) * 2 + x, kq),
    }
    sibling = (sp, y * 2 + 1 - core)
    lanes = [pl.ds(j * W, W) for j in range(PARTS)]
    tables = [
        pltpu.make_async_copy(src, dst, table_sem.at[i])
        for i, (src, dst) in enumerate(zip((lh_hbm, ll_hbm, th_hbm, tl_hbm), (lh, ll, th, tl)))
    ]
    for t in tables:
        t.start()

    barrier = pltpu.get_barrier_semaphore()
    for device in list(partner.values()) + [sibling]:
        pl.semaphore_signal(barrier, inc=1, device_id=device, device_id_type=MESH)
    half, slot = sp // 4, lax.rem(sp, 4)
    holder = [(core * 4 + k, y * 2 + half) for k in range(4)]
    stays = [jnp.logical_and(half == core, slot == k) for k in range(4)]
    for k in range(4):
        @pl.when(jnp.logical_not(stays[k]))
        def _():
            pl.semaphore_signal(barrier, inc=1, device_id=holder[k], device_id_type=MESH)

    pl.semaphore_wait(barrier, 9 - jnp.where(half == core, 1, 0))

    scatter = [
        Scatter(me, partner, part_ref, (p0, p1, p2), "hlx", SPACE_ORDERS[j], lanes[j], ps.at[j], pr_.at[j])
        for j in range(PARTS)
    ]
    gather = [
        Gather(me, partner, spec, DIMS, ORDERS[j][::-1], lanes[j], as_.at[j], ar.at[j]) for j in range(PARTS)
    ]
    for s in scatter:
        s.start(0)

    def kern_copy(k, place):
        return remote(kern_mine.at[:, k], kbuf.at[:, place], ks.at[k], kr_.at[place], holder[k])

    for k in range(4):
        @pl.when(jnp.logical_not(stays[k]))
        def _():
            kern_copy(k, slot).start()

        @pl.when(stays[k])
        def _():
            kbuf[:, slot] = kern_mine[:, k]

    for t in range(3):
        for s in scatter:
            s.finish(t)
            if t < 2:
                s.start(t + 1)
    for j in range(PARTS):
        spec[index(DIMS, me, lanes[j])] = p2[:, lanes[j]]
        gather[j].start(0)
    for t in range(4):
        for g in gather:
            g.finish(t)
            if t < 3:
                g.start(t + 1)
    for k in range(4):
        @pl.when(jnp.logical_not(stays[k]))
        def _():
            kern_copy(k, k).wait_recv()

    def product(i, c):
        rows = pl.ds(pl.multiple_of(i * 64, 64), 64)
        kr, ki = kbuf[0, i], kbuf[1, i]
        value = spec[i // 2, lax.rem(i, 2)].reshape(64, 2 * B)
        sr, si = value[:, :B], value[:, B:]
        ph[rows, :B], pw[rows, :B] = halves(kr * sr - ki * si)
        ph[rows, B:], pw[rows, B:] = halves(kr * si + ki * sr)
        return c

    lax.fori_loop(0, 4, product, 0)
    tables[0].wait()
    tables[1].wait()

    def lift(d, i):
        rows = pl.ds(pl.multiple_of(i * 256, 256), 256)
        return dot3(lh[d, rows, :], ll[d, rows, :], ph[...], pw[...], NT)

    def cross_copy(i):
        return remote(cout.at[i], cin.at[i], xs.at[i], xr.at[i], sibling)

    def lift_other(i, c):
        cout[i] = lift(1 - core, i)
        cross_copy(i).start()
        return c

    lax.fori_loop(0, 4, lift_other, 0)

    def lift_own(i, c):
        rows = pl.ds(pl.multiple_of(i * 256, 256), 256)
        mine = pl.ds(pl.multiple_of(core * C, C), C)
        ch[rows, mine], cl[rows, mine] = halves(lift(core, i))
        return c

    lax.fori_loop(0, 4, lift_own, 0)

    def cross_land(i, c):
        rows = pl.ds(pl.multiple_of(i * 256, 256), 256)
        other = pl.ds(pl.multiple_of((1 - core) * C, C), C)
        cross_copy(i).wait_recv()
        ch[rows, other], cl[rows, other] = halves(cin[i])
        return c

    lax.fori_loop(0, 4, cross_land, 0)
    tables[2].wait()
    tables[3].wait()

    add_light = [
        Scatter(me, partner, light, (l0, l1, l2, l3), DIMS, ORDERS[j], lanes[j], ls.at[j], lr.at[j])
        for j in range(PARTS)
    ]
    spread = [
        Gather(me, partner, slope, DIMS, ORDERS[j][::-1], lanes[j], gs.at[j], gr.at[j]) for j in range(PARTS)
    ]
    own_rows = pl.ds(pl.multiple_of(core * 64 + y * 32, 32), 32)

    def image(j):
        def chunk(i, c):
            top = pl.ds(pl.multiple_of(i * 256, 256), 256)
            low = pl.ds(pl.multiple_of(H + i * 256, 256), 256)
            a = dot3(ch[top, :], cl[top, :], th[j], tl[j], NN)
            b = dot3(ch[low, :], cl[low, :], th[j], tl[j], NN)
            re = a[:, :W] - b[:, W:]
            im = a[:, W:] + b[:, :W]
            field[top, lanes[j]] = re
            field[low, lanes[j]] = im
            light[i, :, :, :, :, lanes[j]] = (re * re + im * im).reshape(2, 2, 2, 32, W)
            return c

        lax.fori_loop(0, 2, chunk, 0)

    def expose(j):
        intensity = l3[:, lanes[j]] * (1.0 / (B * B))
        resist = jax.nn.sigmoid(steepness * (intensity - threshold))
        resist_ref[own_rows, lanes[j]] = resist
        goal = target_ref[own_rows, lanes[j]].astype(jnp.float32)
        slope[index(DIMS, me, lanes[j])] = (4.0 * steepness / (B * B)) * (resist - goal) * resist * (1.0 - resist)

    def back(j):
        def chunk(i, c):
            top = pl.ds(pl.multiple_of(i * 256, 256), 256)
            low = pl.ds(pl.multiple_of(H + i * 256, 256), 256)
            scale = slope[i, :, :, :, :, lanes[j]].reshape(256, W)
            rh, rl = halves(field[top, lanes[j]] * scale)
            ih, il = halves(field[low, lanes[j]] * scale)
            one = dot3(
                th[j], tl[j], jnp.concatenate([rh, ih], 1), jnp.concatenate([rl, il], 1), NT
            )
            two = dot3(
                th[j], tl[j], jnp.concatenate([ih, -rh], 1), jnp.concatenate([il, -rl], 1), NT
            )
            if j == 0:
                grad[:, top] = one
                grad[:, low] = two
            else:
                grad[:, top] = grad[:, top] + one
                grad[:, low] = grad[:, low] + two
            return c

        lax.fori_loop(0, 2, chunk, 0)

    for tick in range(PARTS + 9):
        if tick < PARTS:
            image(tick)
            add_light[tick].start(0)
        for j in range(PARTS):
            s = tick - j
            if 1 <= s <= 4:
                add_light[j].finish(s - 1)
                if s < 4:
                    add_light[j].start(s)
                else:
                    expose(j)
                    spread[j].start(0)
            elif 5 <= s <= 8:
                spread[j].finish(s - 5)
                if s < 8:
                    spread[j].start(s - 4)
        if 0 <= tick - 8 < PARTS:
            back(tick - 8)

    def resist_copy(i, rows, device):
        return remote(resist_ref.at[rows], resist_ref.at[rows], us.at[i], ur.at[i], device)

    row_of = lambda c, yy: pl.ds(pl.multiple_of(c * 64 + yy * 32, 32), 32)
    resist_copy(0, row_of(core, y), partner["y"]).start()
    resist_copy(1, row_of(core, y), sibling).start()

    def grad_copy():
        rows = pl.ds(pl.multiple_of((1 - core) * C, C), C)
        return remote(grad.at[rows], gin, cs, cr, sibling)

    grad_copy().start()

    def adjoint(value, d, first):
        dh, dl = halves(value)

        def chunk(i, c):
            cols = pl.ds(pl.multiple_of(i * 256, 256), 256)
            piece = dot3(dh, dl, lh[d, :, cols], ll[d, :, cols], NN)
            acc[:, cols] = piece if first else acc[:, cols] + piece
            return c

        lax.fori_loop(0, 4, chunk, 0)

    adjoint(grad[pl.ds(pl.multiple_of(core * C, C), C), :], core, True)
    grad_copy().wait_recv()
    adjoint(gin[...], 1 - core, False)

    def combine(i, c):
        rows = pl.ds(pl.multiple_of(i * 64, 64), 64)
        kr, ki = kbuf[0, i], kbuf[1, i]
        pr, pi = acc[rows, :B], acc[rows, B:]
        sums[i // 2, lax.rem(i, 2), :, :, :, :B] = (kr * pr + ki * pi).reshape(2, 2, 16, B)
        sums[i // 2, lax.rem(i, 2), :, :, :, B:] = (kr * pi - ki * pr).reshape(2, 2, 16, B)
        return c

    lax.fori_loop(0, 4, combine, 0)
    add_sums = [
        Scatter(me, partner, sums, (s0, s1, s2, s3), DIMS, ORDERS[j], lanes[j], ss.at[j], sr_.at[j])
        for j in range(PARTS)
    ]
    out_mine = out_ref.at[core]
    deliver = [
        Gather(me, partner, out_mine, DIMS, ORDERS[j][::-1], lanes[j], os_.at[j], or_.at[j]) for j in range(PARTS)
    ]
    for s in add_sums:
        s.start(0)
    for t in range(4):
        for j, s in enumerate(add_sums):
            s.finish(t)
            if t < 3:
                s.start(t + 1)
            else:
                out_ref[(core,) + index(DIMS, me, lanes[j])] = s3[:, lanes[j]]
                deliver[j].start(0)

    def final_copy(j, c):
        view = out_ref.at[(c,) + index(DIMS, {}, lanes[j])]
        return remote(view, view, fs.at[j], fr.at[j], sibling)

    for t in range(4):
        for j, g in enumerate(deliver):
            g.finish(t)
            if t < 3:
                g.start(t + 1)
            else:
                final_copy(j, core).start()
    resist_copy(0, row_of(core, 1 - y), partner["y"]).wait_recv()
    resist_copy(2, row_of(core, 1 - y), sibling).start()
    resist_copy(1, row_of(1 - core, y), sibling).wait_recv()
    resist_copy(2, row_of(1 - core, 1 - y), sibling).wait_recv()
    for j in range(PARTS):
        final_copy(j, 1 - core).wait_recv()

    for j in range(PARTS):
        final_copy(j, core).wait_send()
    for group in (scatter, gather, add_light, spread, add_sums, deliver):
        for one in group:
            one.drain()
    for k in range(4):
        @pl.when(jnp.logical_not(stays[k]))
        def _():
            kern_copy(k, slot).wait_send()

    for i in range(4):
        cross_copy(i).wait_send()
    grad_copy().wait_send()
    resist_copy(0, row_of(core, y), partner["y"]).wait_send()
    resist_copy(1, row_of(core, y), sibling).wait_send()
    resist_copy(2, row_of(core, 1 - y), sibling).wait_send()


def call(kernel, outs, specs, scratch, cid, args, mib):
    vm = pl.BlockSpec(memory_space=pltpu.VMEM)
    return pl.pallas_call(
        kernel,
        out_shape=outs,
        in_specs=specs,
        out_specs=jax.tree.map(lambda _: vm, outs),
        scratch_shapes=scratch,
        compiler_params=pltpu.CompilerParams(
            collective_id=cid, has_side_effects=True, vmem_limit_bytes=mib * 2**20
        ),
    )(*args)


def fast(S, Q, mask, kernels, target):
    f32, bf16 = jnp.float32, jnp.bfloat16
    R = N // S
    DMA = pltpu.SemaphoreType.DMA
    vm, any_ = pl.BlockSpec(memory_space=pltpu.VMEM), pl.BlockSpec(memory_space=pl.ANY)
    high = lax.Precision.HIGH
    sp, kq = lax.axis_index("space"), lax.axis_index("kern")
    table = pixel_table()
    C = B // Q

    rows = jnp.concatenate([lax.dynamic_slice_in_dim(table, part * B + crossed(kq) * C, C, 0) for part in range(2)], axis=0)
    columns = lax.dot_general(rows, mask.astype(f32), (((1,), (1,)), ((), ())), precision=high)
    slab = lax.dynamic_slice_in_dim(table, sp * R, R, 1) * (1.0 / N)
    t = lax.dot_general(columns, slab, (((1,), (1,)), ((), ())), precision=high)
    part = jnp.concatenate([t[:C, :B] - t[C:, B:], t[:C, B:] + t[C:, :B]], axis=1)

    consts = coarse_tables()
    V = pltpu.VMEM
    two = (2, 2, 2, 2)
    total, resist = call(
        imaging_kernel,
        (jax.ShapeDtypeStruct((2,) + two + (16, 2 * B), f32), jax.ShapeDtypeStruct((G // S, G), f32)),
        [vm, vm, vm] + [any_] * 4,
        [V(c.shape, bf16) for c in consts] + [DMA((4,))] + [
            V((2, 4, 64, B), f32),
            V((2, 2, 16, 2 * B), f32), V((2, 16, 2 * B), f32), V((16, 2 * B), f32),
            V(two + (16, 2 * B), f32),
            V((B // 2, 2 * B), bf16), V((B // 2, 2 * B), bf16),
            V((4, 256, B // 2), f32), V((4, 256, B // 2), f32),
            V((G, B), bf16), V((G, B), bf16), V((G, G), f32),
            V(two + (32, G), f32), V((2, 2, 2, 32, G), f32), V((2, 2, 32, G), f32), V((2, 32, G), f32), V((32, G), f32),
            V(two + (32, G), f32),
            V((B, G), f32), V((B // 2, G), f32), V((B // 2, 2 * B), f32),
            V(two + (16, 2 * B), f32), V((2, 2, 2, 16, 2 * B), f32), V((2, 2, 16, 2 * B), f32), V((2, 16, 2 * B), f32),
            V((16, 2 * B), f32),
            DMA((4,)), DMA((4,)), DMA((PARTS, 3)), DMA((PARTS, 3)), DMA((PARTS, 4)), DMA((PARTS, 4)),
            DMA((4,)), DMA((4,)), DMA((PARTS, 4)), DMA((PARTS, 4)), DMA((PARTS, 4)), DMA((PARTS, 4)),
            DMA, DMA, DMA((PARTS, 4)), DMA((PARTS, 4)), DMA((PARTS, 4)), DMA((PARTS, 4)),
            DMA((PARTS,)), DMA((PARTS,)), DMA((3,)), DMA((3,)),
        ],
        1, (part.reshape(2, 2, 2, 16, 2 * B), kernels, target) + consts, 58,
    )

    total = total.reshape(B, 2 * B)
    a, b = slab[:B], slab[B:]
    delta = jnp.concatenate([
        jnp.dot(total, slab, precision=high),
        jnp.dot(total, jnp.concatenate([-b, a], axis=0), precision=high),
    ], axis=0)
    gradient = lax.dot_general(lax.optimization_barrier(delta), table, (((0,), (0,)), ((), ())), precision=high)
    return gradient, resist


def solution(mesh):
    in_specs = (P("space", None), P(None, "kern", "space", None), P("space", None))
    out_specs = (P("space", None), P("space", None))
    S, Q = mesh.shape["space"], mesh.shape["kern"]
    body = functools.partial(fast, S, Q) if (S, Q) == (8, 4) else local
    return jax.shard_map(body, mesh=mesh, in_specs=in_specs, out_specs=out_specs, check_vma=False)
```

```python
import functools

import jax
import jax.numpy as jnp
import ml_dtypes
import numpy as np
from jax import lax
from jax.experimental import pallas as pl
from jax.experimental.pallas import tpu as pltpu
from jax.sharding import PartitionSpec as P

N = 4096
B = 512
G = 1024


steepness = 8.0
threshold = 1.5
highest = lax.Precision.HIGHEST
block_limit = 1024


def phases(left, right, modulus):
    product = left[:, None] * right[None, :] % modulus
    return product.astype(jnp.float32) * (2.0 * jnp.pi / modulus)


def column_table(pixels, frequency, length):
    angle = phases(pixels, frequency, length)
    return jnp.concatenate([jnp.cos(angle), -jnp.sin(angle)], axis=1)


def row_table(pixels, frequency, length):
    angle = phases(pixels, frequency, length)
    return jnp.concatenate([jnp.cos(angle), -jnp.sin(angle)], axis=1) / length


def grid_table(frequency, points):
    angle = phases(frequency, jnp.arange(points, dtype=jnp.int32), points)
    return jnp.concatenate([jnp.cos(angle), jnp.sin(angle)], axis=1)


def forward_columns(mask, frequency):
    rows = mask.shape[0]
    span = min(block_limit, N)
    count = frequency.shape[0]

    def step(index, running):
        start = index * span
        table = column_table(start + jnp.arange(span, dtype=jnp.int32), frequency, N)
        piece = lax.dynamic_slice_in_dim(mask, start, span, 1).astype(jnp.float32)
        return running + lax.dot_general(table, piece, (((0,), (1,)), ((), ())), precision=highest)

    running = lax.fori_loop(0, N // span, step, jnp.zeros((2 * count, rows), jnp.float32))
    return running.reshape(2, count, rows)


def forward_rows(arrived):
    count = arrived.shape[1]
    flat = arrived.reshape(2 * count, N)
    frequency = jnp.arange(B, dtype=jnp.int32) - B // 2
    span = min(block_limit, N)

    def step(index, running):
        start = index * span
        table = row_table(start + jnp.arange(span, dtype=jnp.int32), frequency, N)
        piece = lax.dynamic_slice_in_dim(flat, start, span, 1)
        return running + jnp.dot(piece, table, precision=highest)

    running = lax.fori_loop(0, N // span, step, jnp.zeros((2 * count, 2 * B), jnp.float32))
    real_part = running[:count, :B] - running[count:, B:]
    imag_part = running[:count, B:] + running[count:, :B]
    return jnp.stack([real_part, imag_part])


def adjoint_rows(sum_re, sum_im):
    count = sum_re.shape[0]
    stacked = jnp.concatenate(
        [jnp.concatenate([sum_re, sum_im], axis=1), jnp.concatenate([sum_im, -sum_re], axis=1)],
        axis=0,
    )
    frequency = jnp.arange(B, dtype=jnp.int32) - B // 2
    span = min(block_limit, N)

    def step(index, output):
        start = index * span
        table = row_table(start + jnp.arange(span, dtype=jnp.int32), frequency, N)
        piece = lax.dot_general(stacked, table, (((1,), (1,)), ((), ())), precision=highest)
        return lax.dynamic_update_slice_in_dim(output, piece, start, 1)

    output = lax.fori_loop(0, N // span, step, jnp.zeros((2 * count, N), jnp.float32))
    return output.reshape(2, count, N)


def add_columns(total, spectrum, frequency):
    span = min(block_limit, N)

    def step(index, running):
        start = index * span
        table = column_table(start + jnp.arange(span, dtype=jnp.int32), frequency, N)
        piece = lax.dot_general(spectrum, table, (((0,), (1,)), ((), ())), precision=highest)
        current = lax.dynamic_slice_in_dim(running, start, span, 1)
        return lax.dynamic_update_slice_in_dim(running, current + piece, start, 1)

    return lax.fori_loop(0, N // span, step, total)


def local(mask, kernels, target):
    rows = mask.shape[0]
    kern_count = lax.axis_size("kern")
    space_count = lax.axis_size("space")
    group = lax.axis_index("kern")
    per_space = B // space_count
    per_group = per_space // kern_count
    frequency = jnp.arange(B, dtype=jnp.int32) - B // 2
    subset = (
        per_space * jnp.arange(space_count, dtype=jnp.int32)[:, None]
        + per_group * group
        + jnp.arange(per_group, dtype=jnp.int32)[None, :]
    )
    columns = forward_columns(mask, subset.reshape(-1) - B // 2)
    arrived = lax.all_to_all(columns, "space", split_axis=1, concat_axis=2, tiled=True)
    spectrum = lax.all_gather(forward_rows(arrived), "kern", axis=1, tiled=True)
    kern_swap = jnp.swapaxes(kernels, 1, 2)
    kernel_count = kern_swap.shape[2]
    spec_re = spectrum[0][:, None, :]
    spec_im = spectrum[1][:, None, :]
    prod_re = kern_swap[0] * spec_re - kern_swap[1] * spec_im
    prod_im = kern_swap[0] * spec_im + kern_swap[1] * spec_re
    grid = grid_table(frequency, G)
    lifted = jnp.dot(
        jnp.stack([prod_re, prod_im]).reshape(2 * per_space * kernel_count, B),
        grid,
        precision=highest,
    )
    lifted = lifted.reshape(2, per_space, kernel_count, 2 * G)
    coarse_re = lifted[0, :, :, :G] - lifted[1, :, :, G:]
    coarse_im = lifted[0, :, :, G:] + lifted[1, :, :, :G]
    coarse = jnp.stack([coarse_re, coarse_im], axis=1)
    gathered = lax.all_to_all(coarse, "space", split_axis=3, concat_axis=0, tiled=True)
    grid_rows = gathered.shape[3]
    image = lax.dot_general(
        gathered.reshape(B, 2 * kernel_count * grid_rows),
        grid,
        (((0,), (0,)), ((), ())),
        precision=highest,
    )
    image = image.reshape(2, kernel_count, grid_rows, 2 * G)
    field_re = image[0, :, :, :G] - image[1, :, :, G:]
    field_im = image[0, :, :, G:] + image[1, :, :, :G]
    partial_light = jnp.sum(field_re * field_re + field_im * field_im, axis=0) / (B * B)
    intensity = lax.psum(partial_light, "kern")
    resist = jax.nn.sigmoid(steepness * (intensity - threshold))
    slope = 2.0 * (resist - target.astype(jnp.float32)) * steepness * resist * (1.0 - resist)
    scale = 2.0 * slope / (B * B)
    grad_re = scale * field_re
    grad_im = scale * field_im
    mixed = jnp.stack(
        [
            jnp.concatenate([grad_re, grad_im], axis=-1),
            jnp.concatenate([grad_im, -grad_re], axis=-1),
        ]
    )
    mixed = mixed.reshape(2 * kernel_count * grid_rows, 2 * G)
    backward = lax.dot_general(grid, mixed, (((1,), (1,)), ((), ())), precision=highest)
    backward = backward.reshape(B, 2, kernel_count, grid_rows)
    returned = lax.all_to_all(backward, "space", split_axis=0, concat_axis=3, tiled=True)
    back_re = returned[:, 0]
    back_im = returned[:, 1]
    mixed_two = jnp.stack(
        [
            jnp.concatenate([back_re, back_im], axis=-1),
            jnp.concatenate([back_im, -back_re], axis=-1),
        ]
    )
    mixed_two = mixed_two.reshape(2 * per_space * kernel_count, 2 * G)
    spectral = lax.dot_general(mixed_two, grid, (((1,), (1,)), ((), ())), precision=highest)
    spectral = spectral.reshape(2, per_space, kernel_count, B)
    sum_re = jnp.sum(kern_swap[0] * spectral[0] + kern_swap[1] * spectral[1], axis=1)
    sum_im = jnp.sum(kern_swap[0] * spectral[1] - kern_swap[1] * spectral[0], axis=1)
    empty = jnp.zeros((rows, N), jnp.float32)
    shares = (
        lax.psum_scatter(sum_re, "kern", scatter_dimension=0, tiled=True),
        lax.psum_scatter(sum_im, "kern", scatter_dimension=0, tiled=True),
    )
    delta = adjoint_rows(shares[0], shares[1])
    landed = lax.all_to_all(delta, "space", split_axis=2, concat_axis=1, tiled=True)
    ordering = (
        per_group * jnp.arange(kern_count, dtype=jnp.int32)[:, None, None]
        + per_space * jnp.arange(space_count, dtype=jnp.int32)[None, :, None]
        + jnp.arange(per_group, dtype=jnp.int32)[None, None, :]
    )
    ordered_freq = ordering.reshape(-1) - B // 2
    piece = lax.all_gather(landed, "kern", axis=1, tiled=True)
    width = piece.shape[1]
    gradient = add_columns(empty, piece.reshape(2 * width, rows), ordered_freq)
    return (gradient, resist)


MESH = pl.DeviceIdType.MESH


def split_constant(values):
    high = values.astype(np.float32).astype(ml_dtypes.bfloat16)
    low = (values - high.astype(np.float64)).astype(ml_dtypes.bfloat16)
    return jnp.asarray(high), jnp.asarray(low)


def pixel_tables():
    f = np.arange(B) - B // 2
    angle = (f[:, None] * np.arange(N)) % N * (2 * np.pi / N)
    c, s = np.cos(angle), -np.sin(angle)
    blocks = np.concatenate([c.reshape(B // BLOCK, BLOCK, N), s.reshape(B // BLOCK, BLOCK, N)], 1)
    parity = np.stack([np.concatenate([c[p::2, : N // 2], s[p::2, : N // 2]]) for p in range(2)])
    return split_constant(blocks), split_constant(parity)


def coarse_tables():
    f = np.arange(B) - B // 2
    points = np.arange(G)
    angle = (f[:, None] * points[None, :]) % G * (2 * np.pi / G)
    c, s = np.cos(angle), np.sin(angle)
    order = np.arange(G).reshape(8, 2, 2, G // 32).transpose(1, 2, 0, 3).reshape(2, G // 2)
    lift = np.stack([np.block([[c.T[o], -s.T[o]], [s.T[o], c.T[o]]]) for o in order])
    W = G // STRIPS
    image = np.stack([np.concatenate([c[:, j * W : j * W + W], s[:, j * W : j * W + W]], 1) for j in range(STRIPS)])
    return split_constant(lift) + split_constant(image)


def halves(value):
    high = value.astype(jnp.bfloat16)
    return high, (value - high.astype(jnp.float32)).astype(jnp.bfloat16)


def dot3(ah, al, bh, bl, dims):
    d = functools.partial(lax.dot_general, dimension_numbers=(dims, ((), ())), preferred_element_type=jnp.float32)
    return d(ah, bh) + (d(al, bh) + d(ah, bl))


NN = ((1,), (0,))
NT = ((1,), (1,))
PARTS = 4
BLOCK = 128
STRIPS = 8
STRIP_ORDERS = ("xylh", "ylxh", "lxyh", "xylh", "ylxh", "lxyh", "xylh", "ylxh")
SUM_TIMES = (4, 7, 9, 11)
SPREAD_TIMES = (13, 15, 18, 22)
DIMS = "yhlx"
ORDERS = ("xylh", "ylxh", "lxyh", "xylh")
SPACE_ORDERS = ("xlh", "lxh", "xlh", "lxh")


def remote(src, dst, send, recv, device):
    return pltpu.make_async_remote_copy(
        src_ref=src, dst_ref=dst, send_sem=send, recv_sem=recv, device_id=device, device_id_type=MESH
    )


def crossed(v):
    return 2 * lax.rem(v, 2) + v // 2


def index(dims, fixed, lanes):
    return tuple(fixed.get(d, slice(None)) for d in dims) + (slice(None), lanes)


def without(dims, gone):
    return "".join(d for d in dims if d not in gone)


class Scatter:
    def __init__(self, me, partner, src, bufs, dims, order, lanes, send, recv):
        self.me, self.partner, self.refs, self.dims = me, partner, [src] + list(bufs), dims
        self.order, self.lanes, self.send, self.recv = order, lanes, send, recv

    def copy(self, t):
        d = self.order[t]
        left = without(self.dims, self.order[:t])
        return remote(
            self.refs[t].at[index(left, {d: 1 - self.me[d]}, self.lanes)],
            self.refs[t + 1].at[index(without(left, d), {}, self.lanes)],
            self.send.at[t], self.recv.at[t], self.partner[d],
        )

    def start(self, t):
        self.copy(t).start()

    def finish(self, t):
        self.copy(t).wait_recv()
        d = self.order[t]
        left = without(self.dims, self.order[:t])
        own = self.refs[t][index(left, {d: self.me[d]}, self.lanes)]
        there = index(without(left, d), {}, self.lanes)
        self.refs[t + 1][there] = self.refs[t + 1][there] + own

    def drain(self):
        for t in range(len(self.order)):
            self.copy(t).wait_send()


class Gather:
    def __init__(self, me, partner, ref, dims, order, lanes, send, recv):
        self.me, self.partner, self.ref, self.dims = me, partner, ref, dims
        self.order, self.lanes, self.send, self.recv = order, lanes, send, recv

    def copy(self, t, theirs):
        fixed = {d: self.me[d] for d in self.order[t:]}
        if theirs:
            fixed[self.order[t]] = 1 - fixed[self.order[t]]
        view = self.ref.at[index(self.dims, fixed, self.lanes)]
        return remote(view, view, self.send.at[t], self.recv.at[t], self.partner[self.order[t]])

    def start(self, t):
        self.copy(t, False).start()

    def finish(self, t):
        self.copy(t, True).wait_recv()

    def drain(self):
        for t in range(len(self.order)):
            self.copy(t, False).wait_send()


def imaging_kernel(
    mask_hbm, kern_mine, target_hbm, bh_hbm, bl_hbm, lh_hbm, ll_hbm, th_hbm, tl_hbm,
    out_ref, resist_ref,
    lh, ll, th, tl, table_sem, mbuf, fh, fl, load_sem, slabh, slabl, target_ref, slab_sem, columns, part_ref,
    kbuf, p0, p1, p2, spec, ph, pw, cout, cin, ch, cl, field,
    light, l0, l1, l2, l3, slope, grad, gin, acc, sums, s0, s1, s2, s3,
    ks, kr_, ps, pr_, as_, ar, xs, xr, ls, lr, gs, gr, cs, cr, ss, sr_, os_, or_, fs, fr, us, ur,
):
    H, W, C = G // 2, G // STRIPS, B // 2
    sp, kq = lax.axis_index("space"), lax.axis_index("kern")
    z, x = sp // 2, lax.rem(sp, 2)
    y, core = kq // 2, lax.rem(kq, 2)
    me = {"y": y, "h": z // 2, "l": lax.rem(z, 2), "x": x}
    partner = {
        "y": (sp, (1 - y) * 2 + core),
        "x": (z * 2 + 1 - x, kq),
        "l": ((z + 1 - 2 * me["l"]) * 2 + x, kq),
        "h": (lax.rem(z + 2, 4) * 2 + x, kq),
    }
    sibling = (sp, y * 2 + 1 - core)
    lanes = [pl.ds(j * (2 * B // PARTS), 2 * B // PARTS) for j in range(PARTS)]
    strips = [pl.ds(j * W, W) for j in range(STRIPS)]
    span = N // 4
    loads = []
    for i in range(4):
        cols = pl.ds(i * span, span)
        blk = 2 * core + y
        pairs = [(mask_hbm.at[:, cols], mbuf.at[i]), (bh_hbm.at[blk, :, cols], fh.at[i]), (bl_hbm.at[blk, :, cols], fl.at[i])]
        loads.append([pltpu.make_async_copy(a, b, load_sem.at[i, n]) for n, (a, b) in enumerate(pairs)])
    rows_mine = pl.ds(pl.multiple_of(sp * (N // 8), N // 8), N // 8)
    others = [
        pltpu.make_async_copy(a, b, slab_sem.at[n])
        for n, (a, b) in enumerate(
            [(bh_hbm.at[:, :, rows_mine], slabh), (bl_hbm.at[:, :, rows_mine], slabl), (target_hbm, target_ref)]
        )
    ]
    tables = [
        pltpu.make_async_copy(src, dst, table_sem.at[i])
        for i, (src, dst) in enumerate(zip((lh_hbm, ll_hbm, th_hbm, tl_hbm), (lh, ll, th, tl)))
    ]
    for t in sum(loads, []) + others + tables:
        t.start()

    barrier = pltpu.get_barrier_semaphore()
    for device in list(partner.values()) + [sibling]:
        pl.semaphore_signal(barrier, inc=1, device_id=device, device_id_type=MESH)
    half, slot = sp // 4, lax.rem(sp, 4)
    holder = [(core * 4 + k, y * 2 + half) for k in range(4)]
    stays = [jnp.logical_and(half == core, slot == k) for k in range(4)]
    for k in range(4):
        @pl.when(jnp.logical_not(stays[k]))
        def _():
            pl.semaphore_signal(barrier, inc=1, device_id=holder[k], device_id_type=MESH)

    pl.semaphore_wait(barrier, 9 - jnp.where(half == core, 1, 0))

    scatter = [
        Scatter(me, partner, part_ref, (p0, p1, p2), "hlx", SPACE_ORDERS[j], lanes[j], ps.at[j], pr_.at[j])
        for j in range(PARTS)
    ]
    gather = [
        Gather(me, partner, spec, DIMS, ORDERS[j][::-1], lanes[j], as_.at[j], ar.at[j]) for j in range(PARTS)
    ]
    def kern_copy(k, place):
        return remote(kern_mine.at[:, k], kbuf.at[:, place], ks.at[k], kr_.at[place], holder[k])

    def kern_stay(k):
        return pltpu.make_async_copy(kern_mine.at[:, k], kbuf.at[:, k], kr_.at[k])

    def kern_send(k):
        @pl.when(jnp.logical_not(stays[k]))
        def _():
            kern_copy(k, slot).start()

        @pl.when(stays[k])
        def _():
            kern_stay(k).start()

    kern_send(0)
    kern_send(1)

    for i in range(4):
        for t in loads[i]:
            t.wait()
        m = mbuf[i]
        d = functools.partial(lax.dot_general, dimension_numbers=(NT, ((), ())), preferred_element_type=jnp.float32)
        piece = d(fh[i], m) + d(fl[i], m)
        columns[...] = piece if i == 0 else columns[...] + piece
    for t in others[:2]:
        t.wait()
    colh, coll = halves(columns[...] * (1.0 / N))
    for j in range(PARTS):
        for i in range(2):
            n = j % 2 * 2 + i
            value = dot3(colh, coll, slabh[n], slabl[n], NT)
            if j < 2:
                value = value[:BLOCK, :BLOCK] - value[BLOCK:, BLOCK:]
            else:
                value = value[:BLOCK, BLOCK:] + value[BLOCK:, :BLOCK]
            part_ref[:, :, :, :, pl.ds((2 * j + i) * BLOCK, BLOCK)] = value.reshape(2, 2, 2, 16, BLOCK)
        scatter[j].start(0)
    kern_send(2)

    for t in range(3):
        for s in scatter:
            s.finish(t)
            if t < 2:
                s.start(t + 1)
    for j in range(PARTS):
        spec[index(DIMS, me, lanes[j])] = p2[:, lanes[j]]
        gather[j].start(0)
    kern_send(3)
    for t in range(4):
        for g in gather:
            g.finish(t)
            if t < 3:
                g.start(t + 1)
    for k in range(4):
        @pl.when(jnp.logical_not(stays[k]))
        def _():
            kern_copy(k, k).wait_recv()

        @pl.when(stays[k])
        def _():
            kern_stay(k).wait()

    def product(i, c):
        rows = pl.ds(pl.multiple_of(i * 64, 64), 64)
        kr, ki = kbuf[0, i], kbuf[1, i]
        value = spec[i // 2, lax.rem(i, 2)].reshape(64, 2 * B)
        sr, si = value[:, :B], value[:, B:]
        ph[rows, :B], pw[rows, :B] = halves(kr * sr - ki * si)
        ph[rows, B:], pw[rows, B:] = halves(kr * si + ki * sr)
        return c

    lax.fori_loop(0, 4, product, 0)
    tables[0].wait()
    tables[1].wait()

    def lift(d, i):
        rows = pl.ds(pl.multiple_of(i * 256, 256), 256)
        return dot3(lh[d, rows, :], ll[d, rows, :], ph[...], pw[...], NT)

    def cross_copy(i):
        return remote(cout.at[i], cin.at[i], xs.at[i], xr.at[i], sibling)

    def lift_other(i, c):
        cout[i] = lift(1 - core, i)
        cross_copy(i).start()
        return c

    lax.fori_loop(0, 4, lift_other, 0)

    def lift_own(i, c):
        rows = pl.ds(pl.multiple_of(i * 256, 256), 256)
        mine = pl.ds(pl.multiple_of(core * C, C), C)
        ch[rows, mine], cl[rows, mine] = halves(lift(core, i))
        return c

    lax.fori_loop(0, 4, lift_own, 0)

    def cross_land(i, c):
        rows = pl.ds(pl.multiple_of(i * 256, 256), 256)
        other = pl.ds(pl.multiple_of((1 - core) * C, C), C)
        cross_copy(i).wait_recv()
        ch[rows, other], cl[rows, other] = halves(cin[i])
        return c

    lax.fori_loop(0, 4, cross_land, 0)
    tables[2].wait()
    tables[3].wait()

    add_light = [
        Scatter(me, partner, light, (l0, l1, l2, l3), DIMS, STRIP_ORDERS[j], strips[j], ls.at[j], lr.at[j])
        for j in range(STRIPS)
    ]
    spread = [
        Gather(me, partner, slope, DIMS, STRIP_ORDERS[j][::-1], strips[j], gs.at[j], gr.at[j]) for j in range(STRIPS)
    ]
    own_rows = pl.ds(pl.multiple_of(core * 64 + y * 32, 32), 32)

    def image(j):
        def chunk(i, c):
            top = pl.ds(pl.multiple_of(i * 256, 256), 256)
            low = pl.ds(pl.multiple_of(H + i * 256, 256), 256)
            a = dot3(ch[top, :], cl[top, :], th[j], tl[j], NN)
            b = dot3(ch[low, :], cl[low, :], th[j], tl[j], NN)
            re = a[:, :W] - b[:, W:]
            im = a[:, W:] + b[:, :W]
            field[top, strips[j]] = re
            field[low, strips[j]] = im
            light[i, :, :, :, :, strips[j]] = (re * re + im * im).reshape(2, 2, 2, 32, W)
            return c

        lax.fori_loop(0, 2, chunk, 0)

    def expose(j):
        intensity = l3[:, strips[j]] * (1.0 / (B * B))
        resist = jax.nn.sigmoid(steepness * (intensity - threshold))
        resist_ref[own_rows, strips[j]] = resist
        goal = target_ref[own_rows, strips[j]].astype(jnp.float32)
        slope[index(DIMS, me, strips[j])] = (4.0 * steepness / (B * B)) * (resist - goal) * resist * (1.0 - resist)

    def back(j):
        def chunk(i, c):
            top = pl.ds(pl.multiple_of(i * 256, 256), 256)
            low = pl.ds(pl.multiple_of(H + i * 256, 256), 256)
            scale = slope[i, :, :, :, :, strips[j]].reshape(256, W)
            rh, rl = halves(field[top, strips[j]] * scale)
            ih, il = halves(field[low, strips[j]] * scale)
            one = dot3(
                th[j], tl[j], jnp.concatenate([rh, ih], 1), jnp.concatenate([rl, il], 1), NT
            )
            two = dot3(
                th[j], tl[j], jnp.concatenate([ih, -rh], 1), jnp.concatenate([il, -rl], 1), NT
            )
            if j == 0:
                grad[:, top] = one
                grad[:, low] = two
            else:
                grad[:, top] = grad[:, top] + one
                grad[:, low] = grad[:, low] + two
            return c

        lax.fori_loop(0, 2, chunk, 0)

    def show(j):
        image(j)
        add_light[j].start(0)

    def add_step(j, t):
        add_light[j].finish(t)
        if t < 3:
            add_light[j].start(t + 1)
        else:
            expose(j)
            spread[j].start(0)

    def spread_step(j, t):
        spread[j].finish(t)
        if t < 3:
            spread[j].start(t + 1)
        else:
            back(j)

    events = []
    for j in range(STRIPS):
        events.append((j, 0, j, functools.partial(show, j)))
        for t in range(4):
            events.append((j + SUM_TIMES[t], 2, j, functools.partial(add_step, j, t)))
            events.append((j + SPREAD_TIMES[t], 3 if t == 3 else 1, j, functools.partial(spread_step, j, t)))
    others[2].wait()
    for event in sorted(events, key=lambda e: e[:3]):
        event[3]()

    def resist_copy(i, rows, device):
        return remote(resist_ref.at[rows], resist_ref.at[rows], us.at[i], ur.at[i], device)

    row_of = lambda c, yy: pl.ds(pl.multiple_of(c * 64 + yy * 32, 32), 32)
    resist_copy(0, row_of(core, y), partner["y"]).start()
    resist_copy(1, row_of(core, y), sibling).start()

    def grad_copy():
        rows = pl.ds(pl.multiple_of((1 - core) * C, C), C)
        return remote(grad.at[rows], gin, cs, cr, sibling)

    grad_copy().start()

    def adjoint(dh, dl, d, cols):
        return dot3(dh, dl, lh[d, :, cols], ll[d, :, cols], NN)

    gh, gl = halves(grad[pl.ds(pl.multiple_of(core * C, C), C), :])
    for cols in lanes:
        acc[:, cols] = adjoint(gh, gl, core, cols)
    grad_copy().wait_recv()
    gh, gl = halves(gin[...])
    add_sums = [
        Scatter(me, partner, sums, (s0, s1, s2, s3), DIMS, ORDERS[j], lanes[j], ss.at[j], sr_.at[j])
        for j in range(PARTS)
    ]
    for j in range(2):
        cols = lanes[j]
        pr = acc[:, lanes[j]] + adjoint(gh, gl, 1 - core, lanes[j])
        pi = acc[:, lanes[j + 2]] + adjoint(gh, gl, 1 - core, lanes[j + 2])
        kr = kbuf[0, :, :, lanes[j]].reshape(C, C)
        ki = kbuf[1, :, :, lanes[j]].reshape(C, C)
        sums[:, :, :, :, :, lanes[j]] = (kr * pr + ki * pi).reshape(2, 2, 2, 2, 16, C)
        add_sums[j].start(0)
        sums[:, :, :, :, :, lanes[j + 2]] = (kr * pi - ki * pr).reshape(2, 2, 2, 2, 16, C)
        add_sums[j + 2].start(0)
    out_mine = out_ref.at[core]
    deliver = [
        Gather(me, partner, out_mine, DIMS, ORDERS[j][::-1], lanes[j], os_.at[j], or_.at[j]) for j in range(PARTS)
    ]
    for t in range(4):
        for j, s in enumerate(add_sums):
            s.finish(t)
            if t < 3:
                s.start(t + 1)
            else:
                out_ref[(core,) + index(DIMS, me, lanes[j])] = s3[:, lanes[j]]
                deliver[j].start(0)

    def final_copy(j, c):
        view = out_ref.at[(c,) + index(DIMS, {}, lanes[j])]
        return remote(view, view, fs.at[j], fr.at[j], sibling)

    for t in range(4):
        for j, g in enumerate(deliver):
            g.finish(t)
            if t < 3:
                g.start(t + 1)
            else:
                final_copy(j, core).start()
    resist_copy(0, row_of(core, 1 - y), partner["y"]).wait_recv()
    resist_copy(2, row_of(core, 1 - y), sibling).start()
    resist_copy(1, row_of(1 - core, y), sibling).wait_recv()
    resist_copy(2, row_of(1 - core, 1 - y), sibling).wait_recv()
    for j in range(PARTS):
        final_copy(j, 1 - core).wait_recv()

    for j in range(PARTS):
        final_copy(j, core).wait_send()
    for group in (scatter, gather, add_light, spread, add_sums, deliver):
        for one in group:
            one.drain()
    for k in range(4):
        @pl.when(jnp.logical_not(stays[k]))
        def _():
            kern_copy(k, slot).wait_send()

    for i in range(4):
        cross_copy(i).wait_send()
    grad_copy().wait_send()
    resist_copy(0, row_of(core, y), partner["y"]).wait_send()
    resist_copy(1, row_of(core, y), sibling).wait_send()
    resist_copy(2, row_of(core, 1 - y), sibling).wait_send()


def call(kernel, outs, specs, scratch, cid, args, mib):
    vm = pl.BlockSpec(memory_space=pltpu.VMEM)
    return pl.pallas_call(
        kernel,
        out_shape=outs,
        in_specs=specs,
        out_specs=jax.tree.map(lambda _: vm, outs),
        scratch_shapes=scratch,
        compiler_params=pltpu.CompilerParams(
            collective_id=cid, has_side_effects=True, vmem_limit_bytes=mib * 2**20
        ),
    )(*args)


def final_kernel(
    total_ref, bh_hbm, bl_hbm, eh_hbm, el_hbm, out_hbm, slabh, slabl, eh, el, split, dh, dl, stage, slab_sem, table_sem, out_sem
):
    R, W, H = N // 8, 256, N // 2
    sp = lax.axis_index("space")
    rows = pl.ds(pl.multiple_of(sp * R, R), R)
    slabs = [
        pltpu.make_async_copy(src.at[:, :, rows], dst, slab_sem.at[i])
        for i, (src, dst) in enumerate(((bh_hbm, slabh), (bl_hbm, slabl)))
    ]
    tables = [
        pltpu.make_async_copy(src, dst, table_sem.at[i]) for i, (src, dst) in enumerate(((eh_hbm, eh), (el_hbm, el)))
    ]
    for t in slabs:
        t.start()
    for i in range(2 * B // BLOCK):
        split[i] = total_ref[:, pl.ds(i * BLOCK, BLOCK)] * (1.0 / N)
    for t in slabs:
        t.wait()
    for t in tables:
        t.start()
    sh, sl = slabh[...].reshape(2 * B, R), slabl[...].reshape(2 * B, R)
    groups = B // BLOCK
    for p in range(2):
        re = [split[i, pl.ds(p, B // 2, stride=2), :] for i in range(groups)]
        im = [split[groups + i, pl.ds(p, B // 2, stride=2), :] for i in range(groups)]
        re, im = [halves(v) for v in re], [halves(v) for v in im]
        for side in range(2):
            pick = lambda n: jnp.concatenate(
                sum([[re[i][n], im[i][n]] if side == 0 else [im[i][n], -re[i][n]] for i in range(groups)], []), axis=1
            )
            value = dot3(pick(0), pick(1), sh, sl, NN)
            cols = pl.ds(side * (B // 2), B // 2)
            dh[p, :, cols], dl[p, :, cols] = halves(value.T)
    for t in tables:
        t.wait()

    def out_copy(i, half):
        slot = i % 2
        return pltpu.make_async_copy(
            stage.at[slot, half], out_hbm.at[:, pl.ds(half * H + i * W, W)], out_sem.at[slot, half]
        )

    for i in range(H // W):
        cols = pl.ds(i * W, W)
        even = dot3(dh[0], dl[0], eh[0, :, cols], el[0, :, cols], NN)
        odd = dot3(dh[1], dl[1], eh[1, :, cols], el[1, :, cols], NN)
        for half in range(2):
            if i >= 2:
                out_copy(i - 2, half).wait()
            stage[i % 2, half] = even + odd if half == 0 else even - odd
            out_copy(i, half).start()
    for i in range(H // W - 2, H // W):
        for half in range(2):
            out_copy(i, half).wait()


def fast(S, Q, mask, kernels, target):
    f32, bf16 = jnp.float32, jnp.bfloat16
    R, groups = N // S, B // BLOCK
    DMA = pltpu.SemaphoreType.DMA
    any_ = pl.BlockSpec(memory_space=pl.ANY)
    blocks, parity = pixel_tables()
    consts = coarse_tables()
    V = pltpu.VMEM
    two = (2, 2, 2, 2)
    slab = [V((groups, 2 * BLOCK, R), bf16)] * 2
    total, resist = call(
        imaging_kernel,
        (jax.ShapeDtypeStruct((2,) + two + (16, 2 * B), f32), jax.ShapeDtypeStruct((G // S, G), f32)),
        [any_] * 9,
        [V(c.shape, bf16) for c in consts] + [DMA((4,))] + [
            V((4, R, N // 4), bf16), V((4, 2 * BLOCK, N // 4), bf16), V((4, 2 * BLOCK, N // 4), bf16), DMA((4, 3)),
        ] + slab + [V((G // S, G), jnp.int32), DMA((3,)), V((2 * BLOCK, R), f32), V((2, 2, 2, 16, 2 * B), f32)] + [
            V((2, 4, 64, B), f32),
            V((2, 2, 16, 2 * B), f32), V((2, 16, 2 * B), f32), V((16, 2 * B), f32),
            V(two + (16, 2 * B), f32),
            V((B // 2, 2 * B), bf16), V((B // 2, 2 * B), bf16),
            V((4, 256, B // 2), f32), V((4, 256, B // 2), f32),
            V((G, B), bf16), V((G, B), bf16), V((G, G), f32),
            V(two + (32, G), f32), V((2, 2, 2, 32, G), f32), V((2, 2, 32, G), f32), V((2, 32, G), f32), V((32, G), f32),
            V(two + (32, G), f32),
            V((B, G), f32), V((B // 2, G), f32), V((B // 2, 2 * B), f32),
            V(two + (16, 2 * B), f32), V((2, 2, 2, 16, 2 * B), f32), V((2, 2, 16, 2 * B), f32), V((2, 16, 2 * B), f32),
            V((16, 2 * B), f32),
            DMA((4,)), DMA((4,)), DMA((PARTS, 3)), DMA((PARTS, 3)), DMA((PARTS, 4)), DMA((PARTS, 4)),
            DMA((4,)), DMA((4,)), DMA((STRIPS, 4)), DMA((STRIPS, 4)), DMA((STRIPS, 4)), DMA((STRIPS, 4)),
            DMA, DMA, DMA((PARTS, 4)), DMA((PARTS, 4)), DMA((PARTS, 4)), DMA((PARTS, 4)),
            DMA((PARTS,)), DMA((PARTS,)), DMA((3,)), DMA((3,)),
        ],
        1, (mask, kernels, target) + blocks + consts, 59,
    )
    gradient = pl.pallas_call(
        final_kernel,
        out_shape=jax.ShapeDtypeStruct((R, N), f32),
        in_specs=[pl.BlockSpec(memory_space=pltpu.VMEM)] + [any_] * 4,
        out_specs=any_,
        scratch_shapes=slab + [V(t.shape, bf16) for t in parity] + [
            V((2 * groups, B, BLOCK), f32), V((2, R, B), bf16), V((2, R, B), bf16), V((2, 2, R, 256), f32), DMA((2,)), DMA((2,)), DMA((2, 2)),
        ],
        compiler_params=pltpu.CompilerParams(vmem_limit_bytes=48 * 2**20),
    )(total.reshape(B, 2 * B), *blocks, *parity)
    return gradient, resist


def solution(mesh):
    in_specs = (P("space", None), P(None, "kern", "space", None), P("space", None))
    out_specs = (P("space", None), P("space", None))
    S, Q = mesh.shape["space"], mesh.shape["kern"]
    body = functools.partial(fast, S, Q) if (S, Q) == (8, 4) else local
    return jax.shard_map(body, mesh=mesh, in_specs=in_specs, out_specs=out_specs, check_vma=False)
```

```python
import functools

import jax
import jax.numpy as jnp
import ml_dtypes
import numpy as np
from jax import lax
from jax.experimental import pallas as pl
from jax.experimental.pallas import tpu as pltpu
from jax.sharding import PartitionSpec as P

N = 4096
B = 512
G = 1024


steepness = 8.0
threshold = 1.5
highest = lax.Precision.HIGHEST
block_limit = 1024


def phases(left, right, modulus):
    product = left[:, None] * right[None, :] % modulus
    return product.astype(jnp.float32) * (2.0 * jnp.pi / modulus)


def column_table(pixels, frequency, length):
    angle = phases(pixels, frequency, length)
    return jnp.concatenate([jnp.cos(angle), -jnp.sin(angle)], axis=1)


def row_table(pixels, frequency, length):
    angle = phases(pixels, frequency, length)
    return jnp.concatenate([jnp.cos(angle), -jnp.sin(angle)], axis=1) / length


def grid_table(frequency, points):
    angle = phases(frequency, jnp.arange(points, dtype=jnp.int32), points)
    return jnp.concatenate([jnp.cos(angle), jnp.sin(angle)], axis=1)


def forward_columns(mask, frequency):
    rows = mask.shape[0]
    span = min(block_limit, N)
    count = frequency.shape[0]

    def step(index, running):
        start = index * span
        table = column_table(start + jnp.arange(span, dtype=jnp.int32), frequency, N)
        piece = lax.dynamic_slice_in_dim(mask, start, span, 1).astype(jnp.float32)
        return running + lax.dot_general(table, piece, (((0,), (1,)), ((), ())), precision=highest)

    running = lax.fori_loop(0, N // span, step, jnp.zeros((2 * count, rows), jnp.float32))
    return running.reshape(2, count, rows)


def forward_rows(arrived):
    count = arrived.shape[1]
    flat = arrived.reshape(2 * count, N)
    frequency = jnp.arange(B, dtype=jnp.int32) - B // 2
    span = min(block_limit, N)

    def step(index, running):
        start = index * span
        table = row_table(start + jnp.arange(span, dtype=jnp.int32), frequency, N)
        piece = lax.dynamic_slice_in_dim(flat, start, span, 1)
        return running + jnp.dot(piece, table, precision=highest)

    running = lax.fori_loop(0, N // span, step, jnp.zeros((2 * count, 2 * B), jnp.float32))
    real_part = running[:count, :B] - running[count:, B:]
    imag_part = running[:count, B:] + running[count:, :B]
    return jnp.stack([real_part, imag_part])


def adjoint_rows(sum_re, sum_im):
    count = sum_re.shape[0]
    stacked = jnp.concatenate(
        [jnp.concatenate([sum_re, sum_im], axis=1), jnp.concatenate([sum_im, -sum_re], axis=1)],
        axis=0,
    )
    frequency = jnp.arange(B, dtype=jnp.int32) - B // 2
    span = min(block_limit, N)

    def step(index, output):
        start = index * span
        table = row_table(start + jnp.arange(span, dtype=jnp.int32), frequency, N)
        piece = lax.dot_general(stacked, table, (((1,), (1,)), ((), ())), precision=highest)
        return lax.dynamic_update_slice_in_dim(output, piece, start, 1)

    output = lax.fori_loop(0, N // span, step, jnp.zeros((2 * count, N), jnp.float32))
    return output.reshape(2, count, N)


def add_columns(total, spectrum, frequency):
    span = min(block_limit, N)

    def step(index, running):
        start = index * span
        table = column_table(start + jnp.arange(span, dtype=jnp.int32), frequency, N)
        piece = lax.dot_general(spectrum, table, (((0,), (1,)), ((), ())), precision=highest)
        current = lax.dynamic_slice_in_dim(running, start, span, 1)
        return lax.dynamic_update_slice_in_dim(running, current + piece, start, 1)

    return lax.fori_loop(0, N // span, step, total)


def local(mask, kernels, target):
    rows = mask.shape[0]
    kern_count = lax.axis_size("kern")
    space_count = lax.axis_size("space")
    group = lax.axis_index("kern")
    per_space = B // space_count
    per_group = per_space // kern_count
    frequency = jnp.arange(B, dtype=jnp.int32) - B // 2
    subset = (
        per_space * jnp.arange(space_count, dtype=jnp.int32)[:, None]
        + per_group * group
        + jnp.arange(per_group, dtype=jnp.int32)[None, :]
    )
    columns = forward_columns(mask, subset.reshape(-1) - B // 2)
    arrived = lax.all_to_all(columns, "space", split_axis=1, concat_axis=2, tiled=True)
    spectrum = lax.all_gather(forward_rows(arrived), "kern", axis=1, tiled=True)
    kern_swap = jnp.swapaxes(kernels, 1, 2)
    kernel_count = kern_swap.shape[2]
    spec_re = spectrum[0][:, None, :]
    spec_im = spectrum[1][:, None, :]
    prod_re = kern_swap[0] * spec_re - kern_swap[1] * spec_im
    prod_im = kern_swap[0] * spec_im + kern_swap[1] * spec_re
    grid = grid_table(frequency, G)
    lifted = jnp.dot(
        jnp.stack([prod_re, prod_im]).reshape(2 * per_space * kernel_count, B),
        grid,
        precision=highest,
    )
    lifted = lifted.reshape(2, per_space, kernel_count, 2 * G)
    coarse_re = lifted[0, :, :, :G] - lifted[1, :, :, G:]
    coarse_im = lifted[0, :, :, G:] + lifted[1, :, :, :G]
    coarse = jnp.stack([coarse_re, coarse_im], axis=1)
    gathered = lax.all_to_all(coarse, "space", split_axis=3, concat_axis=0, tiled=True)
    grid_rows = gathered.shape[3]
    image = lax.dot_general(
        gathered.reshape(B, 2 * kernel_count * grid_rows),
        grid,
        (((0,), (0,)), ((), ())),
        precision=highest,
    )
    image = image.reshape(2, kernel_count, grid_rows, 2 * G)
    field_re = image[0, :, :, :G] - image[1, :, :, G:]
    field_im = image[0, :, :, G:] + image[1, :, :, :G]
    partial_light = jnp.sum(field_re * field_re + field_im * field_im, axis=0) / (B * B)
    intensity = lax.psum(partial_light, "kern")
    resist = jax.nn.sigmoid(steepness * (intensity - threshold))
    slope = 2.0 * (resist - target.astype(jnp.float32)) * steepness * resist * (1.0 - resist)
    scale = 2.0 * slope / (B * B)
    grad_re = scale * field_re
    grad_im = scale * field_im
    mixed = jnp.stack(
        [
            jnp.concatenate([grad_re, grad_im], axis=-1),
            jnp.concatenate([grad_im, -grad_re], axis=-1),
        ]
    )
    mixed = mixed.reshape(2 * kernel_count * grid_rows, 2 * G)
    backward = lax.dot_general(grid, mixed, (((1,), (1,)), ((), ())), precision=highest)
    backward = backward.reshape(B, 2, kernel_count, grid_rows)
    returned = lax.all_to_all(backward, "space", split_axis=0, concat_axis=3, tiled=True)
    back_re = returned[:, 0]
    back_im = returned[:, 1]
    mixed_two = jnp.stack(
        [
            jnp.concatenate([back_re, back_im], axis=-1),
            jnp.concatenate([back_im, -back_re], axis=-1),
        ]
    )
    mixed_two = mixed_two.reshape(2 * per_space * kernel_count, 2 * G)
    spectral = lax.dot_general(mixed_two, grid, (((1,), (1,)), ((), ())), precision=highest)
    spectral = spectral.reshape(2, per_space, kernel_count, B)
    sum_re = jnp.sum(kern_swap[0] * spectral[0] + kern_swap[1] * spectral[1], axis=1)
    sum_im = jnp.sum(kern_swap[0] * spectral[1] - kern_swap[1] * spectral[0], axis=1)
    empty = jnp.zeros((rows, N), jnp.float32)
    shares = (
        lax.psum_scatter(sum_re, "kern", scatter_dimension=0, tiled=True),
        lax.psum_scatter(sum_im, "kern", scatter_dimension=0, tiled=True),
    )
    delta = adjoint_rows(shares[0], shares[1])
    landed = lax.all_to_all(delta, "space", split_axis=2, concat_axis=1, tiled=True)
    ordering = (
        per_group * jnp.arange(kern_count, dtype=jnp.int32)[:, None, None]
        + per_space * jnp.arange(space_count, dtype=jnp.int32)[None, :, None]
        + jnp.arange(per_group, dtype=jnp.int32)[None, None, :]
    )
    ordered_freq = ordering.reshape(-1) - B // 2
    piece = lax.all_gather(landed, "kern", axis=1, tiled=True)
    width = piece.shape[1]
    gradient = add_columns(empty, piece.reshape(2 * width, rows), ordered_freq)
    return (gradient, resist)


MESH = pl.DeviceIdType.MESH


def split_constant(values):
    high = values.astype(np.float32).astype(ml_dtypes.bfloat16)
    low = (values - high.astype(np.float64)).astype(ml_dtypes.bfloat16)
    return jnp.asarray(high), jnp.asarray(low)


def pixel_tables():
    f = np.arange(B) - B // 2
    angle = (f[:, None] * np.arange(N)) % N * (2 * np.pi / N)
    c, s = np.cos(angle), -np.sin(angle)
    blocks = np.concatenate([c.reshape(B // BLOCK, BLOCK, N), s.reshape(B // BLOCK, BLOCK, N)], 1)
    parity = np.stack([np.concatenate([c[p::2, : N // 2], s[p::2, : N // 2]]) for p in range(2)])
    return split_constant(blocks), split_constant(parity)


def coarse_tables():
    f = np.arange(B) - B // 2
    points = np.arange(G)
    angle = (f[:, None] * points[None, :]) % G * (2 * np.pi / G)
    c, s = np.cos(angle), np.sin(angle)
    order = np.arange(G).reshape(8, 2, 2, GROUPS, 8).transpose(1, 3, 2, 0, 4).reshape(2, GROUPS, G // 2 // GROUPS)
    lift = np.stack([[np.block([[c.T[o], -s.T[o]], [s.T[o], c.T[o]]]) for o in part] for part in order])
    image = np.concatenate([t[:, i : i + w] for i, w in STRIPS for t in (c, s)], 1)
    return split_constant(lift) + split_constant(image)


def halves(value):
    high = value.astype(jnp.bfloat16)
    return high, (value - high.astype(jnp.float32)).astype(jnp.bfloat16)


def dot3(ah, al, bh, bl, dims):
    d = functools.partial(lax.dot_general, dimension_numbers=(dims, ((), ())), preferred_element_type=jnp.float32)
    return d(ah, bh) + (d(al, bh) + d(ah, bl))


NN = ((1,), (0,))
NT = ((1,), (1,))
PARTS = 4
BLOCK = 128
GROUPS = 4
SUM_BEATS = (5, 8, 10, 12)
SPREAD_BEATS = (14, 16, 19, 22)
STRIPS = ((0, 384), (384, 384), (768, 256))
STRIP_ORDERS = ("xylh", "ylxh", "lxyh")
DIMS = "yhlx"
ORDERS = ("xylh", "ylxh", "lxyh", "xylh")
SPACE_ORDERS = ("xlh", "lxh", "xlh", "lxh")


def remote(src, dst, send, recv, device):
    return pltpu.make_async_remote_copy(
        src_ref=src, dst_ref=dst, send_sem=send, recv_sem=recv, device_id=device, device_id_type=MESH
    )


def crossed(v):
    return 2 * lax.rem(v, 2) + v // 2


def index(dims, fixed, lanes):
    return tuple(fixed.get(d, slice(None)) for d in dims) + (slice(None), lanes)


def without(dims, gone):
    return "".join(d for d in dims if d not in gone)


class Scatter:
    def __init__(self, me, partner, src, bufs, dims, order, lanes, send, recv, base={}):
        self.me, self.partner, self.refs, self.dims, self.base = me, partner, [src] + list(bufs), dims, base
        self.order, self.lanes, self.send, self.recv = order, lanes, send, recv

    def place(self, t, fixed):
        return index(without(self.dims, self.order[:t]), {**self.base, **fixed}, self.lanes)

    def copy(self, t):
        d = self.order[t]
        return remote(
            self.refs[t].at[self.place(t, {d: 1 - self.me[d]})], self.refs[t + 1].at[self.place(t + 1, {})],
            self.send.at[t], self.recv.at[t], self.partner[d],
        )

    def start(self, t):
        self.copy(t).start()

    def finish(self, t):
        self.copy(t).wait_recv()
        d = self.order[t]
        own = self.refs[t][self.place(t, {d: self.me[d]})]
        there = self.place(t + 1, {})
        self.refs[t + 1][there] = self.refs[t + 1][there] + own

    def drain(self):
        for t in range(len(self.order)):
            self.copy(t).wait_send()


class Gather:
    def __init__(self, me, partner, ref, dims, order, lanes, send, recv, base={}):
        self.me, self.partner, self.ref, self.dims, self.base = me, partner, ref, dims, base
        self.order, self.lanes, self.send, self.recv = order, lanes, send, recv

    def copy(self, t, theirs):
        fixed = {**self.base, **{d: self.me[d] for d in self.order[t:]}}
        if theirs:
            fixed[self.order[t]] = 1 - fixed[self.order[t]]
        view = self.ref.at[index(self.dims, fixed, self.lanes)]
        return remote(view, view, self.send.at[t], self.recv.at[t], self.partner[self.order[t]])

    def start(self, t):
        self.copy(t, False).start()

    def finish(self, t):
        self.copy(t, True).wait_recv()

    def drain(self):
        for t in range(len(self.order)):
            self.copy(t, False).wait_send()


def imaging_kernel(
    mask_hbm, kern_mine, target_hbm, bh_hbm, bl_hbm, lh_hbm, ll_hbm, th_hbm, tl_hbm,
    out_ref, resist_ref,
    lh, ll, th, tl, table_sem, mbuf, fh, fl, load_sem, slabh, slabl, target_ref, slab_sem, columns, part_ref,
    kbuf, p0, p1, p2, spec, ph, pw, cout, cin, ch, cl, field, mh, ml,
    light, l0, l1, l2, l3, slope, grad, gin, acc, sums, s0, s1, s2, s3,
    ks, kr_, ps, pr_, as_, ar, xs, xr, ls, lr, gs, gr, cs, cr, ss, sr_, os_, or_, fs, fr, us, ur,
):
    H, C = G // 2 // GROUPS, B // 2
    sp, kq = lax.axis_index("space"), lax.axis_index("kern")
    z, x = sp // 2, lax.rem(sp, 2)
    y, core = kq // 2, lax.rem(kq, 2)
    me = {"y": y, "h": z // 2, "l": lax.rem(z, 2), "x": x}
    partner = {
        "y": (sp, (1 - y) * 2 + core),
        "x": (z * 2 + 1 - x, kq),
        "l": ((z + 1 - 2 * me["l"]) * 2 + x, kq),
        "h": (lax.rem(z + 2, 4) * 2 + x, kq),
    }
    sibling = (sp, y * 2 + 1 - core)
    lanes = [pl.ds(j * (2 * B // PARTS), 2 * B // PARTS) for j in range(PARTS)]
    strips = [pl.ds(i, w) for i, w in STRIPS]
    span = N // 4
    loads = []
    for i in range(4):
        cols = pl.ds(i * span, span)
        blk = 2 * core + y
        pairs = [(mask_hbm.at[:, cols], mbuf.at[i]), (bh_hbm.at[blk, :, cols], fh.at[i]), (bl_hbm.at[blk, :, cols], fl.at[i])]
        loads.append([pltpu.make_async_copy(a, b, load_sem.at[i, n]) for n, (a, b) in enumerate(pairs)])
    rows_mine = pl.ds(pl.multiple_of(sp * (N // 8), N // 8), N // 8)
    others = [
        pltpu.make_async_copy(a, b, slab_sem.at[n])
        for n, (a, b) in enumerate(
            [(bh_hbm.at[:, :, rows_mine], slabh), (bl_hbm.at[:, :, rows_mine], slabl), (target_hbm, target_ref)]
        )
    ]
    tables = [
        pltpu.make_async_copy(src, dst, table_sem.at[i])
        for i, (src, dst) in enumerate(zip((lh_hbm, ll_hbm, th_hbm, tl_hbm), (lh, ll, th, tl)))
    ]
    for t in sum(loads, []) + others + tables:
        t.start()

    barrier = pltpu.get_barrier_semaphore()
    for device in list(partner.values()) + [sibling]:
        pl.semaphore_signal(barrier, inc=1, device_id=device, device_id_type=MESH)
    half, slot = sp // 4, lax.rem(sp, 4)
    stays = jnp.logical_and(half == core, x == core)
    kinds = [lax.rem(2 * (1 - half) + i, 4) for i in range(4)]
    leaves = [jnp.logical_not(jnp.logical_and(stays, k == z)) for k in kinds]
    comes = [jnp.logical_not(jnp.logical_and(stays, slot == i)) for i in range(4)]
    for i in range(4):
        @pl.when(comes[i])
        def _():
            pl.semaphore_signal(barrier, inc=1, device_id=(core * 4 + i, y * 2 + x), device_id_type=MESH)

    pl.semaphore_wait(barrier, 9 - jnp.where(stays, 1, 0))

    scatter = [
        Scatter(me, partner, part_ref, (p0, p1, p2), "hlx", SPACE_ORDERS[j], lanes[j], ps.at[j], pr_.at[j])
        for j in range(PARTS)
    ]
    gather = [
        Gather(me, partner, spec, DIMS, ORDERS[j][::-1], lanes[j], as_.at[j], ar.at[j]) for j in range(PARTS)
    ]
    def kern_copy(i, place):
        k = kinds[i]
        return remote(
            kern_mine.at[:, k], kbuf.at[:, place], ks.at[i], kr_.at[place], (2 * k + core, y * 2 + half)
        )

    def kern_stay():
        return pltpu.make_async_copy(kern_mine.at[:, z], kbuf.at[:, slot], kr_.at[slot])

    def kern_send(i):
        @pl.when(leaves[i])
        def _():
            kern_copy(i, slot).start()

    @pl.when(stays)
    def _():
        kern_stay().start()

    for i in range(4):
        kern_send(i)
    for i in range(4):
        for t in loads[i]:
            t.wait()
        m = mbuf[i]
        d = functools.partial(lax.dot_general, dimension_numbers=(NT, ((), ())), preferred_element_type=jnp.float32)
        piece = d(fh[i], m) + d(fl[i], m)
        columns[...] = piece if i == 0 else columns[...] + piece
    for t in others[:2]:
        t.wait()
    colh, coll = halves(columns[...] * (1.0 / N))
    for j in range(PARTS):
        for i in range(2):
            n = j % 2 * 2 + i
            value = dot3(colh, coll, slabh[n], slabl[n], NT)
            if j < 2:
                value = value[:BLOCK, :BLOCK] - value[BLOCK:, BLOCK:]
            else:
                value = value[:BLOCK, BLOCK:] + value[BLOCK:, :BLOCK]
            part_ref[:, :, :, :, pl.ds((2 * j + i) * BLOCK, BLOCK)] = value.reshape(2, 2, 2, 16, BLOCK)
        scatter[j].start(0)

    for t in range(3):
        for s in scatter:
            s.finish(t)
            if t < 2:
                s.start(t + 1)
    for j in range(PARTS):
        spec[index(DIMS, me, lanes[j])] = p2[:, lanes[j]]
        gather[j].start(0)
    for t in range(4):
        for g in gather:
            g.finish(t)
            if t < 3:
                g.start(t + 1)
    for i in range(4):
        @pl.when(comes[i])
        def _():
            kern_copy(0, i).wait_recv()

    @pl.when(stays)
    def _():
        kern_stay().wait()

    def product(i, c):
        rows = pl.ds(pl.multiple_of(i * 64, 64), 64)
        kr, ki = kbuf[0, i], kbuf[1, i]
        value = spec[i // 2, lax.rem(i, 2)].reshape(64, 2 * B)
        sr, si = value[:, :B], value[:, B:]
        ph[rows, :B], pw[rows, :B] = halves(kr * sr - ki * si)
        ph[rows, B:], pw[rows, B:] = halves(kr * si + ki * sr)
        return c

    lax.fori_loop(0, 4, product, 0)

    mine = pl.ds(pl.multiple_of(core * C, C), C)
    other = pl.ds(pl.multiple_of((1 - core) * C, C), C)

    def lift(d, g):
        return dot3(lh[d, g], ll[d, g], ph[...], pw[...], NT)

    def cross_copy(g):
        return remote(cout.at[g], cin.at[g], xs.at[g], xr.at[g], sibling)

    def lift_other(g):
        cout[g] = lift(1 - core, g)
        cross_copy(g).start()

    def lift_own(g):
        ch[g, :, mine], cl[g, :, mine] = halves(lift(core, g))

    def cross_land(g):
        cross_copy(g).wait_recv()
        ch[g, :, other], cl[g, :, other] = halves(cin[g])

    def add_light(g):
        return [
            Scatter(
                me, partner, light, (l0, l1, l2, l3), "g" + DIMS, o, strips[i], ls.at[g, i], lr.at[g, i], {"g": g}
            )
            for i, o in enumerate(STRIP_ORDERS)
        ]

    def spread(g):
        return [
            Gather(me, partner, slope, "g" + DIMS, o[::-1], strips[i], gs.at[g, i], gr.at[g, i], {"g": g})
            for i, o in enumerate(STRIP_ORDERS)
        ]

    def image(g, i):
        start, w = STRIPS[i]
        cols = pl.ds(2 * start, 2 * w)
        value = dot3(ch[g], cl[g], th[:, cols], tl[:, cols], NN)
        re = value[:H, :w] - value[H:, w:]
        im = value[:H, w:] + value[H:, :w]
        field[g, :H, strips[i]] = re
        field[g, H:, strips[i]] = im
        light[g, :, :, :, :, :, strips[i]] = (re * re + im * im).reshape(2, 2, 2, 2, 8, w)

    def expose(g, i):
        rows = pl.ds(pl.multiple_of(core * 64 + y * 32 + g * 8, 8), 8)
        intensity = l3[g, :, strips[i]] * (1.0 / (B * B))
        resist = jax.nn.sigmoid(steepness * (intensity - threshold))
        resist_ref[rows, strips[i]] = resist
        goal = target_ref[rows, strips[i]].astype(jnp.float32)
        slope[index("g" + DIMS, {**me, "g": g}, strips[i])] = (
            (4.0 * steepness / (B * B)) * (resist - goal) * resist * (1.0 - resist)
        )

    def back(g):
        for i, (start, w) in enumerate(STRIPS):
            scale = slope[g, :, :, :, :, :, strips[i]].reshape(H, w)
            rh, rl = halves(field[g, :H, strips[i]] * scale)
            ih, il = halves(field[g, H:, strips[i]] * scale)
            one, two = pl.ds(2 * start, w), pl.ds(2 * start + w, w)
            mh[:H, one], mh[:H, two], mh[H:, one], mh[H:, two] = rh, ih, ih, -rh
            ml[:H, one], ml[:H, two], ml[H:, one], ml[H:, two] = rl, il, il, -rl

    def back_rows(g, rows):
        grad[g, rows, :] = dot3(th[rows, :], tl[rows, :], mh[...], ml[...], NT)

    def grad_copy(g):
        return remote(grad.at[g, other], gin.at[g], cs.at[g], cr.at[g], sibling)

    def adjoint(value, d, g):
        dh, dl = halves(value)
        return dot3(dh, dl, lh[d, g], ll[d, g], NN)

    def adjoint_own(g):
        acc[...] = acc[...] + adjoint(grad[g, mine, :], core, g)

    def adjoint_land(g):
        grad_copy(g).wait_recv()
        acc[...] = acc[...] + adjoint(gin[g], 1 - core, g)

    def show(g, i):
        if i == 0:
            lift_own(g)

            @pl.when(g < GROUPS - 1)
            def _():
                lift_other(g + 1)

            cross_land(g)
        image(g, i)
        add_light(g)[i].start(0)

    def add_step(n, g, i):
        s = add_light(g)[i]
        s.finish(n)
        if n < 3:
            s.start(n + 1)
        else:
            expose(g, i)
            spread(g)[i].start(0)

    def spread_step(n, g, i):
        s = spread(g)[i]
        s.finish(n)
        if n < 3:
            s.start(n + 1)

    def back_first(g, i):
        back(g)
        back_rows(g, other)
        grad_copy(g).start()

    def back_second(g, i):
        back_rows(g, mine)

    def back_third(g, i):
        adjoint_own(g)

        @pl.when(g > 0)
        def _():
            adjoint_land(g - 1)

    items = []
    stages = [(0, 1, show)]
    stages += [(SUM_BEATS[n], 2, functools.partial(add_step, n)) for n in range(4)]
    stages += [(SPREAD_BEATS[n], -1 if n == 3 else 0, functools.partial(spread_step, n)) for n in range(4)]
    last = SPREAD_BEATS[3] + 2
    stages += [(last, 0, back_first), (last + 1, 0, back_second), (last + 2, 0, back_third)]
    for beat, rank, body in stages:
        for i in range(len(STRIPS) if beat < last else 1):
            items.append(((beat + i) % len(STRIPS), rank, -beat, (beat + i) // len(STRIPS), i, body))
    items.sort(key=lambda e: e[:3])
    ticks = GROUPS + max(e[3] for e in items)

    def tick(t, c):
        for _, _, _, late, i, body in items:
            g = t - late

            @pl.when(jnp.logical_and(g >= 0, g < GROUPS))
            def _():
                body(g, i)

        return c

    for t in tables + others[2:]:
        t.wait()
    acc[...] = jnp.zeros_like(acc)
    lift_other(0)
    lax.fori_loop(0, ticks, tick, 0)

    def resist_copy(i, rows, device):
        return remote(resist_ref.at[rows], resist_ref.at[rows], us.at[i], ur.at[i], device)

    row_of = lambda c, yy: pl.ds(pl.multiple_of(c * 64 + yy * 32, 32), 32)
    resist_copy(0, row_of(core, y), partner["y"]).start()
    resist_copy(1, row_of(core, y), sibling).start()

    grad_copy(GROUPS - 1).wait_recv()
    gh, gl = halves(gin[GROUPS - 1])
    far = lambda cols: dot3(gh, gl, lh[1 - core, GROUPS - 1, :, cols], ll[1 - core, GROUPS - 1, :, cols], NN)
    add_sums = [
        Scatter(me, partner, sums, (s0, s1, s2, s3), DIMS, ORDERS[j], lanes[j], ss.at[j], sr_.at[j])
        for j in range(PARTS)
    ]
    for j in range(2):
        pr = acc[:, lanes[j]] + far(lanes[j])
        pi = acc[:, lanes[j + 2]] + far(lanes[j + 2])
        kr = kbuf[0, :, :, lanes[j]].reshape(C, C)
        ki = kbuf[1, :, :, lanes[j]].reshape(C, C)
        sums[:, :, :, :, :, lanes[j]] = (kr * pr + ki * pi).reshape(2, 2, 2, 2, 16, C)
        add_sums[j].start(0)
        sums[:, :, :, :, :, lanes[j + 2]] = (kr * pi - ki * pr).reshape(2, 2, 2, 2, 16, C)
        add_sums[j + 2].start(0)
    out_mine = out_ref.at[core]
    deliver = [
        Gather(me, partner, out_mine, DIMS, ORDERS[j][::-1], lanes[j], os_.at[j], or_.at[j]) for j in range(PARTS)
    ]
    for t in range(4):
        for j, s in enumerate(add_sums):
            s.finish(t)
            if t < 3:
                s.start(t + 1)
            else:
                out_ref[(core,) + index(DIMS, me, lanes[j])] = s3[:, lanes[j]]
                deliver[j].start(0)

    def final_copy(j, c):
        view = out_ref.at[(c,) + index(DIMS, {}, lanes[j])]
        return remote(view, view, fs.at[j], fr.at[j], sibling)

    for t in range(4):
        for j, g in enumerate(deliver):
            g.finish(t)
            if t < 3:
                g.start(t + 1)
            else:
                final_copy(j, core).start()
    resist_copy(0, row_of(core, 1 - y), partner["y"]).wait_recv()
    resist_copy(2, row_of(core, 1 - y), sibling).start()
    resist_copy(1, row_of(1 - core, y), sibling).wait_recv()
    resist_copy(2, row_of(1 - core, 1 - y), sibling).wait_recv()
    for j in range(PARTS):
        final_copy(j, 1 - core).wait_recv()

    for j in range(PARTS):
        final_copy(j, core).wait_send()
    for group in (scatter, gather, add_sums, deliver):
        for one in group:
            one.drain()

    def drain(g, c):
        for one in add_light(g) + spread(g):
            one.drain()
        cross_copy(g).wait_send()
        grad_copy(g).wait_send()
        return c

    lax.fori_loop(0, GROUPS, drain, 0)
    for i in range(4):
        @pl.when(leaves[i])
        def _():
            kern_copy(i, slot).wait_send()

    resist_copy(0, row_of(core, y), partner["y"]).wait_send()
    resist_copy(1, row_of(core, y), sibling).wait_send()
    resist_copy(2, row_of(core, 1 - y), sibling).wait_send()


def call(kernel, outs, specs, scratch, cid, args, mib):
    vm = pl.BlockSpec(memory_space=pltpu.VMEM)
    return pl.pallas_call(
        kernel,
        out_shape=outs,
        in_specs=specs,
        out_specs=jax.tree.map(lambda _: vm, outs),
        scratch_shapes=scratch,
        compiler_params=pltpu.CompilerParams(
            collective_id=cid, has_side_effects=True, vmem_limit_bytes=mib * 2**20
        ),
    )(*args)


def final_kernel(
    total_ref, bh_hbm, bl_hbm, eh_hbm, el_hbm, out_hbm, slabh, slabl, eh, el, split, dh, dl, stage, slab_sem, table_sem, out_sem
):
    R, W, H = N // 8, 256, N // 2
    sp = lax.axis_index("space")
    rows = pl.ds(pl.multiple_of(sp * R, R), R)
    slabs = [
        pltpu.make_async_copy(src.at[:, :, rows], dst, slab_sem.at[i])
        for i, (src, dst) in enumerate(((bh_hbm, slabh), (bl_hbm, slabl)))
    ]
    tables = [
        pltpu.make_async_copy(src, dst, table_sem.at[i]) for i, (src, dst) in enumerate(((eh_hbm, eh), (el_hbm, el)))
    ]
    for t in slabs:
        t.start()
    for i in range(2 * B // BLOCK):
        split[i] = total_ref[:, pl.ds(i * BLOCK, BLOCK)] * (1.0 / N)
    for t in slabs:
        t.wait()
    for t in tables:
        t.start()
    sh, sl = slabh[...].reshape(2 * B, R), slabl[...].reshape(2 * B, R)
    groups = B // BLOCK
    for p in range(2):
        re = [split[i, pl.ds(p, B // 2, stride=2), :] for i in range(groups)]
        im = [split[groups + i, pl.ds(p, B // 2, stride=2), :] for i in range(groups)]
        re, im = [halves(v) for v in re], [halves(v) for v in im]
        for side in range(2):
            pick = lambda n: jnp.concatenate(
                sum([[re[i][n], im[i][n]] if side == 0 else [im[i][n], -re[i][n]] for i in range(groups)], []), axis=1
            )
            value = dot3(pick(0), pick(1), sh, sl, NN)
            cols = pl.ds(side * (B // 2), B // 2)
            dh[p, :, cols], dl[p, :, cols] = halves(value.T)
    for t in tables:
        t.wait()

    def out_copy(i, half):
        slot = i % 2
        return pltpu.make_async_copy(
            stage.at[slot, half], out_hbm.at[:, pl.ds(half * H + i * W, W)], out_sem.at[slot, half]
        )

    for i in range(H // W):
        cols = pl.ds(i * W, W)
        even = dot3(dh[0], dl[0], eh[0, :, cols], el[0, :, cols], NN)
        odd = dot3(dh[1], dl[1], eh[1, :, cols], el[1, :, cols], NN)
        for half in range(2):
            if i >= 2:
                out_copy(i - 2, half).wait()
            stage[i % 2, half] = even + odd if half == 0 else even - odd
            out_copy(i, half).start()
    for i in range(H // W - 2, H // W):
        for half in range(2):
            out_copy(i, half).wait()


def fast(S, Q, mask, kernels, target):
    f32, bf16 = jnp.float32, jnp.bfloat16
    R, groups = N // S, B // BLOCK
    DMA = pltpu.SemaphoreType.DMA
    any_ = pl.BlockSpec(memory_space=pl.ANY)
    blocks, parity = pixel_tables()
    consts = coarse_tables()
    V = pltpu.VMEM
    two = (2, 2, 2, 2)
    slab = [V((groups, 2 * BLOCK, R), bf16)] * 2
    total, resist = call(
        imaging_kernel,
        (jax.ShapeDtypeStruct((2,) + two + (16, 2 * B), f32), jax.ShapeDtypeStruct((G // S, G), f32)),
        [any_] * 9,
        [V(c.shape, bf16) for c in consts] + [DMA((4,))] + [
            V((4, R, N // 4), bf16), V((4, 2 * BLOCK, N // 4), bf16), V((4, 2 * BLOCK, N // 4), bf16), DMA((4, 3)),
        ] + slab + [V((G // S, G), jnp.int32), DMA((3,)), V((2 * BLOCK, R), f32), V((2, 2, 2, 16, 2 * B), f32)] + [
            V((2, 4, 64, B), f32),
            V((2, 2, 16, 2 * B), f32), V((2, 16, 2 * B), f32), V((16, 2 * B), f32),
            V(two + (16, 2 * B), f32),
            V((B // 2, 2 * B), bf16), V((B // 2, 2 * B), bf16),
            V((4, 256, B // 2), f32), V((4, 256, B // 2), f32),
            V((GROUPS, G // GROUPS, B), bf16), V((GROUPS, G // GROUPS, B), bf16), V((GROUPS, G // GROUPS, G), f32),
            V((G // GROUPS, 2 * G), bf16), V((G // GROUPS, 2 * G), bf16),
            V((GROUPS,) + two + (8, G), f32), V((GROUPS, 2, 2, 2, 8, G), f32), V((GROUPS, 2, 2, 8, G), f32),
            V((GROUPS, 2, 8, G), f32), V((GROUPS, 8, G), f32),
            V((GROUPS,) + two + (8, G), f32),
            V((GROUPS, B, G // GROUPS), f32), V((GROUPS, B // 2, G // GROUPS), f32), V((B // 2, 2 * B), f32),
            V(two + (16, 2 * B), f32), V((2, 2, 2, 16, 2 * B), f32), V((2, 2, 16, 2 * B), f32), V((2, 16, 2 * B), f32),
            V((16, 2 * B), f32),
            DMA((4,)), DMA((4,)), DMA((PARTS, 3)), DMA((PARTS, 3)), DMA((PARTS, 4)), DMA((PARTS, 4)),
            DMA((4,)), DMA((4,))] + [DMA((GROUPS, len(STRIPS), 4))] * 4 + [
            DMA((GROUPS,)), DMA((GROUPS,)), DMA((PARTS, 4)), DMA((PARTS, 4)), DMA((PARTS, 4)), DMA((PARTS, 4)),
            DMA((PARTS,)), DMA((PARTS,)), DMA((3,)), DMA((3,)),
        ],
        1, (mask, kernels, target) + blocks + consts, 59,
    )
    gradient = pl.pallas_call(
        final_kernel,
        out_shape=jax.ShapeDtypeStruct((R, N), f32),
        in_specs=[pl.BlockSpec(memory_space=pltpu.VMEM)] + [any_] * 4,
        out_specs=any_,
        scratch_shapes=slab + [V(t.shape, bf16) for t in parity] + [
            V((2 * groups, B, BLOCK), f32), V((2, R, B), bf16), V((2, R, B), bf16), V((2, 2, R, 256), f32), DMA((2,)), DMA((2,)), DMA((2, 2)),
        ],
        compiler_params=pltpu.CompilerParams(vmem_limit_bytes=48 * 2**20),
    )(total.reshape(B, 2 * B), *blocks, *parity)
    return gradient, resist


def solution(mesh):
    in_specs = (P("space", None), P(None, "kern", "space", None), P("space", None))
    out_specs = (P("space", None), P("space", None))
    S, Q = mesh.shape["space"], mesh.shape["kern"]
    body = functools.partial(fast, S, Q) if (S, Q) == (8, 4) else local
    return jax.shard_map(body, mesh=mesh, in_specs=in_specs, out_specs=out_specs, check_vma=False)
```

```python
import functools

import jax
import jax.numpy as jnp
import ml_dtypes
import numpy as np
from jax import lax
from jax.experimental import pallas as pl
from jax.experimental.pallas import tpu as pltpu
from jax.sharding import PartitionSpec as P

N = 4096
B = 512
G = 1024


steepness = 8.0
threshold = 1.5
highest = lax.Precision.HIGHEST
block_limit = 1024


def phases(left, right, modulus):
    product = left[:, None] * right[None, :] % modulus
    return product.astype(jnp.float32) * (2.0 * jnp.pi / modulus)


def column_table(pixels, frequency, length):
    angle = phases(pixels, frequency, length)
    return jnp.concatenate([jnp.cos(angle), -jnp.sin(angle)], axis=1)


def row_table(pixels, frequency, length):
    angle = phases(pixels, frequency, length)
    return jnp.concatenate([jnp.cos(angle), -jnp.sin(angle)], axis=1) / length


def grid_table(frequency, points):
    angle = phases(frequency, jnp.arange(points, dtype=jnp.int32), points)
    return jnp.concatenate([jnp.cos(angle), jnp.sin(angle)], axis=1)


def forward_columns(mask, frequency):
    rows = mask.shape[0]
    span = min(block_limit, N)
    count = frequency.shape[0]

    def step(index, running):
        start = index * span
        table = column_table(start + jnp.arange(span, dtype=jnp.int32), frequency, N)
        piece = lax.dynamic_slice_in_dim(mask, start, span, 1).astype(jnp.float32)
        return running + lax.dot_general(table, piece, (((0,), (1,)), ((), ())), precision=highest)

    running = lax.fori_loop(0, N // span, step, jnp.zeros((2 * count, rows), jnp.float32))
    return running.reshape(2, count, rows)


def forward_rows(arrived):
    count = arrived.shape[1]
    flat = arrived.reshape(2 * count, N)
    frequency = jnp.arange(B, dtype=jnp.int32) - B // 2
    span = min(block_limit, N)

    def step(index, running):
        start = index * span
        table = row_table(start + jnp.arange(span, dtype=jnp.int32), frequency, N)
        piece = lax.dynamic_slice_in_dim(flat, start, span, 1)
        return running + jnp.dot(piece, table, precision=highest)

    running = lax.fori_loop(0, N // span, step, jnp.zeros((2 * count, 2 * B), jnp.float32))
    real_part = running[:count, :B] - running[count:, B:]
    imag_part = running[:count, B:] + running[count:, :B]
    return jnp.stack([real_part, imag_part])


def adjoint_rows(sum_re, sum_im):
    count = sum_re.shape[0]
    stacked = jnp.concatenate(
        [jnp.concatenate([sum_re, sum_im], axis=1), jnp.concatenate([sum_im, -sum_re], axis=1)],
        axis=0,
    )
    frequency = jnp.arange(B, dtype=jnp.int32) - B // 2
    span = min(block_limit, N)

    def step(index, output):
        start = index * span
        table = row_table(start + jnp.arange(span, dtype=jnp.int32), frequency, N)
        piece = lax.dot_general(stacked, table, (((1,), (1,)), ((), ())), precision=highest)
        return lax.dynamic_update_slice_in_dim(output, piece, start, 1)

    output = lax.fori_loop(0, N // span, step, jnp.zeros((2 * count, N), jnp.float32))
    return output.reshape(2, count, N)


def add_columns(total, spectrum, frequency):
    span = min(block_limit, N)

    def step(index, running):
        start = index * span
        table = column_table(start + jnp.arange(span, dtype=jnp.int32), frequency, N)
        piece = lax.dot_general(spectrum, table, (((0,), (1,)), ((), ())), precision=highest)
        current = lax.dynamic_slice_in_dim(running, start, span, 1)
        return lax.dynamic_update_slice_in_dim(running, current + piece, start, 1)

    return lax.fori_loop(0, N // span, step, total)


def local(mask, kernels, target):
    rows = mask.shape[0]
    kern_count = lax.axis_size("kern")
    space_count = lax.axis_size("space")
    group = lax.axis_index("kern")
    per_space = B // space_count
    per_group = per_space // kern_count
    frequency = jnp.arange(B, dtype=jnp.int32) - B // 2
    subset = (
        per_space * jnp.arange(space_count, dtype=jnp.int32)[:, None]
        + per_group * group
        + jnp.arange(per_group, dtype=jnp.int32)[None, :]
    )
    columns = forward_columns(mask, subset.reshape(-1) - B // 2)
    arrived = lax.all_to_all(columns, "space", split_axis=1, concat_axis=2, tiled=True)
    spectrum = lax.all_gather(forward_rows(arrived), "kern", axis=1, tiled=True)
    kern_swap = jnp.swapaxes(kernels, 1, 2)
    kernel_count = kern_swap.shape[2]
    spec_re = spectrum[0][:, None, :]
    spec_im = spectrum[1][:, None, :]
    prod_re = kern_swap[0] * spec_re - kern_swap[1] * spec_im
    prod_im = kern_swap[0] * spec_im + kern_swap[1] * spec_re
    grid = grid_table(frequency, G)
    lifted = jnp.dot(
        jnp.stack([prod_re, prod_im]).reshape(2 * per_space * kernel_count, B),
        grid,
        precision=highest,
    )
    lifted = lifted.reshape(2, per_space, kernel_count, 2 * G)
    coarse_re = lifted[0, :, :, :G] - lifted[1, :, :, G:]
    coarse_im = lifted[0, :, :, G:] + lifted[1, :, :, :G]
    coarse = jnp.stack([coarse_re, coarse_im], axis=1)
    gathered = lax.all_to_all(coarse, "space", split_axis=3, concat_axis=0, tiled=True)
    grid_rows = gathered.shape[3]
    image = lax.dot_general(
        gathered.reshape(B, 2 * kernel_count * grid_rows),
        grid,
        (((0,), (0,)), ((), ())),
        precision=highest,
    )
    image = image.reshape(2, kernel_count, grid_rows, 2 * G)
    field_re = image[0, :, :, :G] - image[1, :, :, G:]
    field_im = image[0, :, :, G:] + image[1, :, :, :G]
    partial_light = jnp.sum(field_re * field_re + field_im * field_im, axis=0) / (B * B)
    intensity = lax.psum(partial_light, "kern")
    resist = jax.nn.sigmoid(steepness * (intensity - threshold))
    slope = 2.0 * (resist - target.astype(jnp.float32)) * steepness * resist * (1.0 - resist)
    scale = 2.0 * slope / (B * B)
    grad_re = scale * field_re
    grad_im = scale * field_im
    mixed = jnp.stack(
        [
            jnp.concatenate([grad_re, grad_im], axis=-1),
            jnp.concatenate([grad_im, -grad_re], axis=-1),
        ]
    )
    mixed = mixed.reshape(2 * kernel_count * grid_rows, 2 * G)
    backward = lax.dot_general(grid, mixed, (((1,), (1,)), ((), ())), precision=highest)
    backward = backward.reshape(B, 2, kernel_count, grid_rows)
    returned = lax.all_to_all(backward, "space", split_axis=0, concat_axis=3, tiled=True)
    back_re = returned[:, 0]
    back_im = returned[:, 1]
    mixed_two = jnp.stack(
        [
            jnp.concatenate([back_re, back_im], axis=-1),
            jnp.concatenate([back_im, -back_re], axis=-1),
        ]
    )
    mixed_two = mixed_two.reshape(2 * per_space * kernel_count, 2 * G)
    spectral = lax.dot_general(mixed_two, grid, (((1,), (1,)), ((), ())), precision=highest)
    spectral = spectral.reshape(2, per_space, kernel_count, B)
    sum_re = jnp.sum(kern_swap[0] * spectral[0] + kern_swap[1] * spectral[1], axis=1)
    sum_im = jnp.sum(kern_swap[0] * spectral[1] - kern_swap[1] * spectral[0], axis=1)
    empty = jnp.zeros((rows, N), jnp.float32)
    shares = (
        lax.psum_scatter(sum_re, "kern", scatter_dimension=0, tiled=True),
        lax.psum_scatter(sum_im, "kern", scatter_dimension=0, tiled=True),
    )
    delta = adjoint_rows(shares[0], shares[1])
    landed = lax.all_to_all(delta, "space", split_axis=2, concat_axis=1, tiled=True)
    ordering = (
        per_group * jnp.arange(kern_count, dtype=jnp.int32)[:, None, None]
        + per_space * jnp.arange(space_count, dtype=jnp.int32)[None, :, None]
        + jnp.arange(per_group, dtype=jnp.int32)[None, None, :]
    )
    ordered_freq = ordering.reshape(-1) - B // 2
    piece = lax.all_gather(landed, "kern", axis=1, tiled=True)
    width = piece.shape[1]
    gradient = add_columns(empty, piece.reshape(2 * width, rows), ordered_freq)
    return (gradient, resist)


MESH = pl.DeviceIdType.MESH


def split_constant(values):
    high = values.astype(np.float32).astype(ml_dtypes.bfloat16)
    low = (values - high.astype(np.float64)).astype(ml_dtypes.bfloat16)
    return jnp.asarray(high), jnp.asarray(low)


def pixel_tables():
    f = np.arange(B) - B // 2
    angle = (f[:, None] * np.arange(N)) % N * (2 * np.pi / N)
    c, s = np.cos(angle), -np.sin(angle)
    blocks = np.concatenate([c.reshape(B // BLOCK, BLOCK, N), s.reshape(B // BLOCK, BLOCK, N)], 1)
    parity = np.stack([np.concatenate([c[p::2, : N // 2], s[p::2, : N // 2]]) for p in range(2)])
    return split_constant(blocks), split_constant(parity)


def coarse_tables():
    f = np.arange(B) - B // 2
    points = np.arange(G)
    angle = (f[:, None] * points[None, :]) % G * (2 * np.pi / G)
    c, s = np.cos(angle), np.sin(angle)
    order = np.arange(G).reshape(8, 2, 2, GROUPS, 8).transpose(1, 3, 2, 0, 4).reshape(2, GROUPS, G // 2 // GROUPS)
    lift = np.stack([[np.block([[c.T[o], -s.T[o]], [s.T[o], c.T[o]]]) for o in part] for part in order])
    image = np.concatenate([t[:, i : i + w] for i, w in STRIPS for t in (c, s)], 1)
    return split_constant(lift) + split_constant(image)


def halves(value):
    high = value.astype(jnp.bfloat16)
    return high, (value - high.astype(jnp.float32)).astype(jnp.bfloat16)


def dot3(ah, al, bh, bl, dims):
    d = functools.partial(lax.dot_general, dimension_numbers=(dims, ((), ())), preferred_element_type=jnp.float32)
    both, rows = d(jnp.concatenate([ah, al], axis=0), bh), ah.shape[0]
    return both[:rows] + (both[rows:] + d(ah, bl))


NN = ((1,), (0,))
NT = ((1,), (1,))
PARTS = 4
BLOCK = 128
GROUPS = 4
SUM_BEATS = (5, 8, 10, 12)
SPREAD_BEATS = (14, 16, 19, 22)
STRIPS = ((0, 384), (384, 384), (768, 256))
STRIP_ORDERS = ("xylh", "ylxh", "lxyh")
DIMS = "yhlx"
PLANE_ORDERS = ("xy", "yx", "xy", "yx")
SPACE_ORDERS = ("xlh", "lxh", "xlh", "lxh")


def remote(src, dst, send, recv, device):
    return pltpu.make_async_remote_copy(
        src_ref=src, dst_ref=dst, send_sem=send, recv_sem=recv, device_id=device, device_id_type=MESH
    )


def crossed(v):
    return 2 * lax.rem(v, 2) + v // 2


def index(dims, fixed, lanes):
    return tuple(fixed.get(d, slice(None)) for d in dims) + (slice(None), lanes)


def without(dims, gone):
    return "".join(d for d in dims if d not in gone)


class Scatter:
    def __init__(self, me, partner, src, bufs, dims, order, lanes, send, recv, base={}):
        self.me, self.partner, self.refs, self.dims, self.base = me, partner, [src] + list(bufs), dims, base
        self.order, self.lanes, self.send, self.recv = order, lanes, send, recv

    def place(self, t, fixed):
        return index(without(self.dims, self.order[:t]), {**self.base, **fixed}, self.lanes)

    def copy(self, t):
        d = self.order[t]
        return remote(
            self.refs[t].at[self.place(t, {d: 1 - self.me[d]})], self.refs[t + 1].at[self.place(t + 1, {})],
            self.send.at[t], self.recv.at[t], self.partner[d],
        )

    def start(self, t):
        self.copy(t).start()

    def finish(self, t):
        self.copy(t).wait_recv()
        d = self.order[t]
        own = self.refs[t][self.place(t, {d: self.me[d]})]
        there = self.place(t + 1, {})
        self.refs[t + 1][there] = self.refs[t + 1][there] + own

    def drain(self):
        for t in range(len(self.order)):
            self.copy(t).wait_send()


class Gather:
    def __init__(self, me, partner, ref, dims, order, lanes, send, recv, base={}):
        self.me, self.partner, self.ref, self.dims, self.base = me, partner, ref, dims, base
        self.order, self.lanes, self.send, self.recv = order, lanes, send, recv

    def copy(self, t, theirs):
        fixed = {**self.base, **{d: self.me[d] for d in self.order[t:]}}
        if theirs:
            fixed[self.order[t]] = 1 - fixed[self.order[t]]
        view = self.ref.at[index(self.dims, fixed, self.lanes)]
        return remote(view, view, self.send.at[t], self.recv.at[t], self.partner[self.order[t]])

    def start(self, t):
        self.copy(t, False).start()

    def finish(self, t):
        self.copy(t, True).wait_recv()

    def drain(self):
        for t in range(len(self.order)):
            self.copy(t, False).wait_send()


def imaging_kernel(
    mask_hbm, kern_mine, target_hbm, bh_hbm, bl_hbm, lh_hbm, ll_hbm, th_hbm, tl_hbm,
    out_ref, resist_ref,
    lh, ll, th, tl, table_sem, mbuf, fh, fl, load_sem, slabh, slabl, target_ref, slab_sem, columns, part_ref,
    kbuf, p0, p1, p2, spec, ph, pw, cout, cin, ch, cl, field, mh, ml,
    light, l0, l1, l2, l3, slope, grad, gin, acc, sums, s0, s1, s2,
    ks, kr_, ps, pr_, as_, ar, xs, xr, ls, lr, gs, gr, cs, cr, ss, sr_, os_, or_, fs, fr, us, ur, zs, zr,
):
    H, C = G // 2 // GROUPS, B // 2
    sp, kq = lax.axis_index("space"), lax.axis_index("kern")
    z, x = sp // 2, lax.rem(sp, 2)
    y, core = kq // 2, lax.rem(kq, 2)
    me = {"y": y, "h": z // 2, "l": lax.rem(z, 2), "x": x}
    partner = {
        "y": (sp, (1 - y) * 2 + core),
        "x": (z * 2 + 1 - x, kq),
        "l": ((z + 1 - 2 * me["l"]) * 2 + x, kq),
        "h": (lax.rem(z + 2, 4) * 2 + x, kq),
    }
    sibling = (sp, y * 2 + 1 - core)
    lanes = [pl.ds(j * (2 * B // PARTS), 2 * B // PARTS) for j in range(PARTS)]
    strips = [pl.ds(i, w) for i, w in STRIPS]
    span = N // 4

    def loads(i):
        cols = pl.ds(pl.multiple_of(i * span, span), span)
        blk = 2 * core + y
        pairs = [(mask_hbm.at[:, cols], mbuf.at[i]), (bh_hbm.at[blk, :, cols], fh.at[i]), (bl_hbm.at[blk, :, cols], fl.at[i])]
        return [pltpu.make_async_copy(a, b, load_sem.at[i, n]) for n, (a, b) in enumerate(pairs)]

    rows_mine = pl.ds(pl.multiple_of(sp * (N // 8), N // 8), N // 8)
    others = [
        pltpu.make_async_copy(a, b, slab_sem.at[n])
        for n, (a, b) in enumerate(
            [(bh_hbm.at[:, :, rows_mine], slabh), (bl_hbm.at[:, :, rows_mine], slabl), (target_hbm, target_ref)]
        )
    ]
    tables = [
        pltpu.make_async_copy(src, dst, table_sem.at[i])
        for i, (src, dst) in enumerate(zip((lh_hbm, ll_hbm, th_hbm, tl_hbm), (lh, ll, th, tl)))
    ]
    for t in sum([loads(i) for i in range(4)], []) + others:
        t.start()

    far_z = [lax.rem(z + o, 4) for o in range(1, 4)]

    def z_copy(use, j, src, dst, to, slot):
        return remote(src, dst, zs.at[use, j, to], zr.at[use, j, slot], (to * 2 + x, kq))

    def z_block(ref, j, zz):
        return ref.at[index(DIMS, {"y": y, "x": x, "h": zz // 2, "l": lax.rem(zz, 2)}, lanes[j])]

    def z_spread(use, ref, j):
        return [z_copy(use, j, z_block(ref, j, z), z_block(ref, j, z), zz, z) for zz in far_z]

    def z_spread_land(use, ref, j):
        for zz in far_z:
            z_copy(use, j, z_block(ref, j, zz), z_block(ref, j, zz), zz, zz).wait_recv()

    barrier = pltpu.get_barrier_semaphore()
    for device in list(partner.values()) + [sibling, ((3 - z) * 2 + x, kq)]:
        pl.semaphore_signal(barrier, inc=1, device_id=device, device_id_type=MESH)
    half, slot = sp // 4, lax.rem(sp, 4)
    stays = jnp.logical_and(half == core, x == core)
    kinds = [lax.rem(2 * (1 - half) + i, 4) for i in range(4)]
    leaves = [jnp.logical_not(jnp.logical_and(stays, k == z)) for k in kinds]
    comes = [jnp.logical_not(jnp.logical_and(stays, slot == i)) for i in range(4)]
    for i in range(4):
        @pl.when(comes[i])
        def _():
            pl.semaphore_signal(barrier, inc=1, device_id=(core * 4 + i, y * 2 + x), device_id_type=MESH)

    pl.semaphore_wait(barrier, 10 - jnp.where(stays, 1, 0))

    scatter = [
        Scatter(me, partner, part_ref, (p0, p1, p2), "hlx", SPACE_ORDERS[j], lanes[j], ps.at[j], pr_.at[j])
        for j in range(PARTS)
    ]
    gather = [
        Gather(me, partner, spec, DIMS, PLANE_ORDERS[j][::-1], lanes[j], as_.at[j], ar.at[j]) for j in range(PARTS)
    ]
    def kern_copy(i, place):
        k = kinds[i]
        return remote(
            kern_mine.at[:, k], kbuf.at[:, place], ks.at[i], kr_.at[place], (2 * k + core, y * 2 + half)
        )

    def kern_stay():
        return pltpu.make_async_copy(kern_mine.at[:, z], kbuf.at[:, slot], kr_.at[slot])

    def kern_send(i):
        @pl.when(leaves[i])
        def _():
            kern_copy(i, slot).start()

    @pl.when(stays)
    def _():
        kern_stay().start()

    for i in range(4):
        kern_send(i)
    columns[...] = jnp.zeros_like(columns)

    def sweep(i, c):
        for t in loads(i):
            t.wait()
        m = mbuf[i]
        d = functools.partial(lax.dot_general, dimension_numbers=(NT, ((), ())), preferred_element_type=jnp.float32)
        both = d(jnp.concatenate([fh[i], fl[i]], axis=0), m)
        columns[...] += both[: 2 * BLOCK] + both[2 * BLOCK :]
        return c

    lax.fori_loop(0, 4, sweep, 0)
    for t in tables:
        t.start()
    for t in others[:2]:
        t.wait()
    colh, coll = halves(columns[...] * (1.0 / N))

    def band(n, c):
        value = dot3(colh, coll, slabh[n], slabl[n], NT)
        re = value[:BLOCK, :BLOCK] - value[BLOCK:, BLOCK:]
        im = value[:BLOCK, BLOCK:] + value[BLOCK:, :BLOCK]
        at = pl.multiple_of(n * BLOCK, BLOCK)
        part_ref[:, :, :, :, pl.ds(at, BLOCK)] = re.reshape(2, 2, 2, 16, BLOCK)
        part_ref[:, :, :, :, pl.ds(B + at, BLOCK)] = im.reshape(2, 2, 2, 16, BLOCK)
        return c

    lax.fori_loop(0, B // BLOCK, band, 0)
    for one in scatter:
        one.start(0)

    for t in range(3):
        for s in scatter:
            s.finish(t)
            if t < 2:
                s.start(t + 1)
    for j in range(PARTS):
        spec[index(DIMS, me, lanes[j])] = p2[:, lanes[j]]
        for one in z_spread(0, spec, j):
            one.start()
    for j, g in enumerate(gather):
        z_spread_land(0, spec, j)
        g.start(0)
    for t in range(2):
        for g in gather:
            g.finish(t)
            if t < 1:
                g.start(t + 1)
    for i in range(4):
        @pl.when(comes[i])
        def _():
            kern_copy(0, i).wait_recv()

    @pl.when(stays)
    def _():
        kern_stay().wait()

    def product(i, c):
        rows = pl.ds(pl.multiple_of(i * 64, 64), 64)
        kr, ki = kbuf[0, i], kbuf[1, i]
        value = spec[i // 2, lax.rem(i, 2)].reshape(64, 2 * B)
        sr, si = value[:, :B], value[:, B:]
        ph[rows, :B], pw[rows, :B] = halves(kr * sr - ki * si)
        ph[rows, B:], pw[rows, B:] = halves(kr * si + ki * sr)
        return c

    lax.fori_loop(0, 4, product, 0)

    mine = pl.ds(pl.multiple_of(core * C, C), C)
    other = pl.ds(pl.multiple_of((1 - core) * C, C), C)

    def lift(d, g):
        return dot3(lh[d, g], ll[d, g], ph[...], pw[...], NT)

    def cross_copy(g):
        return remote(cout.at[g], cin.at[g], xs.at[g], xr.at[g], sibling)

    def lift_other(g):
        cout[g] = lift(1 - core, g)
        cross_copy(g).start()

    def lift_own(g):
        ch[g, :, mine], cl[g, :, mine] = halves(lift(core, g))

    def cross_land(g):
        cross_copy(g).wait_recv()
        ch[g, :, other], cl[g, :, other] = halves(cin[g])

    def add_light(g):
        return [
            Scatter(
                me, partner, light, (l0, l1, l2, l3), "g" + DIMS, o, strips[i], ls.at[g, i], lr.at[g, i], {"g": g}
            )
            for i, o in enumerate(STRIP_ORDERS)
        ]

    def spread(g):
        return [
            Gather(me, partner, slope, "g" + DIMS, o[::-1], strips[i], gs.at[g, i], gr.at[g, i], {"g": g})
            for i, o in enumerate(STRIP_ORDERS)
        ]

    def image(g, i):
        start, w = STRIPS[i]
        cols = pl.ds(2 * start, 2 * w)
        value = dot3(ch[g], cl[g], th[:, cols], tl[:, cols], NN)
        re = value[:H, :w] - value[H:, w:]
        im = value[:H, w:] + value[H:, :w]
        field[g, :H, strips[i]] = re
        field[g, H:, strips[i]] = im
        light[g, :, :, :, :, :, strips[i]] = (re * re + im * im).reshape(2, 2, 2, 2, 8, w)

    def expose(g, i):
        rows = pl.ds(pl.multiple_of(core * 64 + y * 32 + g * 8, 8), 8)
        intensity = l3[g, :, strips[i]] * (1.0 / (B * B))
        resist = jax.nn.sigmoid(steepness * (intensity - threshold))
        resist_ref[rows, strips[i]] = resist
        goal = target_ref[rows, strips[i]].astype(jnp.float32)
        slope[index("g" + DIMS, {**me, "g": g}, strips[i])] = (
            (4.0 * steepness / (B * B)) * (resist - goal) * resist * (1.0 - resist)
        )

    def back(g):
        for i, (start, w) in enumerate(STRIPS):
            scale = slope[g, :, :, :, :, :, strips[i]].reshape(H, w)
            rh, rl = halves(field[g, :H, strips[i]] * scale)
            ih, il = halves(field[g, H:, strips[i]] * scale)
            one, two = pl.ds(2 * start, w), pl.ds(2 * start + w, w)
            mh[:H, one], mh[:H, two], mh[H:, one], mh[H:, two] = rh, ih, ih, -rh
            ml[:H, one], ml[:H, two], ml[H:, one], ml[H:, two] = rl, il, il, -rl

    def back_rows(g, rows):
        grad[g, rows, :] = dot3(th[rows, :], tl[rows, :], mh[...], ml[...], NT)

    def grad_copy(g):
        return remote(grad.at[g, other], gin.at[g], cs.at[g], cr.at[g], sibling)

    def adjoint(value, d, g):
        dh, dl = halves(value)
        return dot3(dh, dl, lh[d, g], ll[d, g], NN)

    def adjoint_own(g):
        acc[...] = acc[...] + adjoint(grad[g, mine, :], core, g)

    def adjoint_land(g):
        grad_copy(g).wait_recv()
        acc[...] = acc[...] + adjoint(gin[g], 1 - core, g)

    def show(g, i):
        if i == 0:
            lift_own(g)

            @pl.when(g < GROUPS - 1)
            def _():
                lift_other(g + 1)

            cross_land(g)
        image(g, i)
        add_light(g)[i].start(0)

    def add_step(n, g, i):
        s = add_light(g)[i]
        s.finish(n)
        if n < 3:
            s.start(n + 1)
        else:
            expose(g, i)
            spread(g)[i].start(0)

    def spread_step(n, g, i):
        s = spread(g)[i]
        s.finish(n)
        if n < 3:
            s.start(n + 1)

    def back_first(g, i):
        back(g)
        back_rows(g, other)
        grad_copy(g).start()

    def back_second(g, i):
        back_rows(g, mine)

    def back_third(g, i):
        adjoint_own(g)

        @pl.when(g > 0)
        def _():
            adjoint_land(g - 1)

    items = []
    stages = [(0, 1, show)]
    stages += [(SUM_BEATS[n], 2, functools.partial(add_step, n)) for n in range(4)]
    stages += [(SPREAD_BEATS[n], -1 if n == 3 else 0, functools.partial(spread_step, n)) for n in range(4)]
    last = SPREAD_BEATS[3] + 2
    stages += [(last, 0, back_first), (last + 1, 0, back_second), (last + 2, 0, back_third)]
    for beat, rank, body in stages:
        for i in range(len(STRIPS) if beat < last else 1):
            items.append(((beat + i) % len(STRIPS), rank, -beat, (beat + i) // len(STRIPS), i, body))
    items.sort(key=lambda e: e[:3])
    ticks = GROUPS + max(e[3] for e in items)

    def tick(t, c):
        for _, _, _, late, i, body in items:
            g = t - late

            @pl.when(jnp.logical_and(g >= 0, g < GROUPS))
            def _():
                body(g, i)

        return c

    for t in tables + others[2:]:
        t.wait()
    acc[...] = jnp.zeros_like(acc)
    lift_other(0)
    lax.fori_loop(0, ticks, tick, 0)

    def resist_copy(i, rows, device):
        return remote(resist_ref.at[rows], resist_ref.at[rows], us.at[i], ur.at[i], device)

    row_of = lambda c, yy: pl.ds(pl.multiple_of(c * 64 + yy * 32, 32), 32)
    resist_copy(0, row_of(core, y), partner["y"]).start()
    resist_copy(1, row_of(core, y), sibling).start()

    grad_copy(GROUPS - 1).wait_recv()
    gh, gl = halves(gin[GROUPS - 1])
    far = lambda cols: dot3(gh, gl, lh[1 - core, GROUPS - 1, :, cols], ll[1 - core, GROUPS - 1, :, cols], NN)
    add_sums = [
        Scatter(me, partner, sums, (s0, s1), DIMS, PLANE_ORDERS[j], lanes[j], ss.at[j], sr_.at[j])
        for j in range(PARTS)
    ]
    for j in range(2):
        pr = acc[:, lanes[j]] + far(lanes[j])
        pi = acc[:, lanes[j + 2]] + far(lanes[j + 2])
        kr = kbuf[0, :, :, lanes[j]].reshape(C, C)
        ki = kbuf[1, :, :, lanes[j]].reshape(C, C)
        sums[:, :, :, :, :, lanes[j]] = (kr * pr + ki * pi).reshape(2, 2, 2, 2, 16, C)
        add_sums[j].start(0)
        sums[:, :, :, :, :, lanes[j + 2]] = (kr * pi - ki * pr).reshape(2, 2, 2, 2, 16, C)
        add_sums[j + 2].start(0)
    out_mine = out_ref.at[core]
    deliver = [
        Gather(me, partner, out_mine, DIMS, PLANE_ORDERS[j][::-1], lanes[j], os_.at[j], or_.at[j])
        for j in range(PARTS)
    ]

    def part_of(j, zz):
        return s1.at[zz // 2, lax.rem(zz, 2), :, lanes[j]]

    def z_send(j, zz):
        return z_copy(1, j, part_of(j, zz), s2.at[z, :, lanes[j]], zz, z)

    for j, s in enumerate(add_sums):
        s.finish(0)
        s.start(1)
    for j, s in enumerate(add_sums):
        s.finish(1)
        for zz in far_z:
            z_send(j, zz).start()
    for j in range(PARTS):
        value = s1[me["h"], me["l"], :, lanes[j]]
        for zz in far_z:
            z_copy(1, j, part_of(j, zz), s2.at[zz, :, lanes[j]], zz, zz).wait_recv()
            value = value + s2[zz, :, lanes[j]]
        out_ref[(core,) + index(DIMS, me, lanes[j])] = value
        for one in z_spread(2, out_mine, j):
            one.start()

    def final_copy(j, c):
        view = out_ref.at[(c,) + index(DIMS, {}, lanes[j])]
        return remote(view, view, fs.at[j], fr.at[j], sibling)

    for j, g in enumerate(deliver):
        z_spread_land(2, out_mine, j)
        g.start(0)
    for t in range(2):
        for j, g in enumerate(deliver):
            g.finish(t)
            if t < 1:
                g.start(t + 1)
            else:
                final_copy(j, core).start()
    resist_copy(0, row_of(core, 1 - y), partner["y"]).wait_recv()
    resist_copy(2, row_of(core, 1 - y), sibling).start()
    resist_copy(1, row_of(1 - core, y), sibling).wait_recv()
    resist_copy(2, row_of(1 - core, 1 - y), sibling).wait_recv()
    for j in range(PARTS):
        final_copy(j, 1 - core).wait_recv()

    for j in range(PARTS):
        final_copy(j, core).wait_send()
    for j in range(PARTS):
        for one in z_spread(0, spec, j) + [z_send(j, zz) for zz in far_z] + z_spread(2, out_mine, j):
            one.wait_send()
    for group in (scatter, gather, add_sums, deliver):
        for one in group:
            one.drain()

    def drain(g, c):
        for one in add_light(g) + spread(g):
            one.drain()
        cross_copy(g).wait_send()
        grad_copy(g).wait_send()
        return c

    lax.fori_loop(0, GROUPS, drain, 0)
    for i in range(4):
        @pl.when(leaves[i])
        def _():
            kern_copy(i, slot).wait_send()

    resist_copy(0, row_of(core, y), partner["y"]).wait_send()
    resist_copy(1, row_of(core, y), sibling).wait_send()
    resist_copy(2, row_of(core, 1 - y), sibling).wait_send()


def call(kernel, outs, specs, scratch, cid, args, mib):
    vm = pl.BlockSpec(memory_space=pltpu.VMEM)
    return pl.pallas_call(
        kernel,
        out_shape=outs,
        in_specs=specs,
        out_specs=jax.tree.map(lambda _: vm, outs),
        scratch_shapes=scratch,
        compiler_params=pltpu.CompilerParams(
            collective_id=cid, has_side_effects=True, vmem_limit_bytes=mib * 2**20
        ),
    )(*args)


def final_kernel(
    total_ref, bh_hbm, bl_hbm, eh_hbm, el_hbm, out_hbm, slabh, slabl, eh, el, split, dh, dl, stage, slab_sem, table_sem, out_sem
):
    R, W, H = N // 8, 256, N // 2
    sp = lax.axis_index("space")
    rows = pl.ds(pl.multiple_of(sp * R, R), R)
    slabs = [
        pltpu.make_async_copy(src.at[:, :, rows], dst, slab_sem.at[i])
        for i, (src, dst) in enumerate(((bh_hbm, slabh), (bl_hbm, slabl)))
    ]
    tables = [
        pltpu.make_async_copy(src, dst, table_sem.at[i]) for i, (src, dst) in enumerate(((eh_hbm, eh), (el_hbm, el)))
    ]
    for t in slabs:
        t.start()
    for i in range(2 * B // BLOCK):
        split[i] = total_ref[:, pl.ds(i * BLOCK, BLOCK)] * (1.0 / N)
    for t in slabs:
        t.wait()
    for t in tables:
        t.start()
    sh, sl = slabh[...].reshape(2 * B, R), slabl[...].reshape(2 * B, R)
    groups = B // BLOCK
    for p in range(2):
        re = [split[i, pl.ds(p, B // 2, stride=2), :] for i in range(groups)]
        im = [split[groups + i, pl.ds(p, B // 2, stride=2), :] for i in range(groups)]
        re, im = [halves(v) for v in re], [halves(v) for v in im]
        for side in range(2):
            pick = lambda n: jnp.concatenate(
                sum([[re[i][n], im[i][n]] if side == 0 else [im[i][n], -re[i][n]] for i in range(groups)], []), axis=1
            )
            value = dot3(pick(0), pick(1), sh, sl, NN)
            cols = pl.ds(side * (B // 2), B // 2)
            dh[p, :, cols], dl[p, :, cols] = halves(value.T)
    for t in tables:
        t.wait()

    def out_copy(i, half):
        slot = i % 2
        return pltpu.make_async_copy(
            stage.at[slot, half], out_hbm.at[:, pl.ds(half * H + i * W, W)], out_sem.at[slot, half]
        )

    for i in range(H // W):
        cols = pl.ds(i * W, W)
        even = dot3(dh[0], dl[0], eh[0, :, cols], el[0, :, cols], NN)
        odd = dot3(dh[1], dl[1], eh[1, :, cols], el[1, :, cols], NN)
        for half in range(2):
            if i >= 2:
                out_copy(i - 2, half).wait()
            stage[i % 2, half] = even + odd if half == 0 else even - odd
            out_copy(i, half).start()
    for i in range(H // W - 2, H // W):
        for half in range(2):
            out_copy(i, half).wait()


def fast(S, Q, mask, kernels, target):
    f32, bf16 = jnp.float32, jnp.bfloat16
    R, groups = N // S, B // BLOCK
    DMA = pltpu.SemaphoreType.DMA
    any_ = pl.BlockSpec(memory_space=pl.ANY)
    blocks, parity = pixel_tables()
    consts = coarse_tables()
    V = pltpu.VMEM
    two = (2, 2, 2, 2)
    slab = [V((groups, 2 * BLOCK, R), bf16)] * 2
    total, resist = call(
        imaging_kernel,
        (jax.ShapeDtypeStruct((2,) + two + (16, 2 * B), f32), jax.ShapeDtypeStruct((G // S, G), f32)),
        [any_] * 9,
        [V(c.shape, bf16) for c in consts] + [DMA((4,))] + [
            V((4, R, N // 4), bf16), V((4, 2 * BLOCK, N // 4), bf16), V((4, 2 * BLOCK, N // 4), bf16), DMA((4, 3)),
        ] + slab + [V((G // S, G), jnp.int32), DMA((3,)), V((2 * BLOCK, R), f32), V((2, 2, 2, 16, 2 * B), f32)] + [
            V((2, 4, 64, B), f32),
            V((2, 2, 16, 2 * B), f32), V((2, 16, 2 * B), f32), V((16, 2 * B), f32),
            V(two + (16, 2 * B), f32),
            V((B // 2, 2 * B), bf16), V((B // 2, 2 * B), bf16),
            V((4, 256, B // 2), f32), V((4, 256, B // 2), f32),
            V((GROUPS, G // GROUPS, B), bf16), V((GROUPS, G // GROUPS, B), bf16), V((GROUPS, G // GROUPS, G), f32),
            V((G // GROUPS, 2 * G), bf16), V((G // GROUPS, 2 * G), bf16),
            V((GROUPS,) + two + (8, G), f32), V((GROUPS, 2, 2, 2, 8, G), f32), V((GROUPS, 2, 2, 8, G), f32),
            V((GROUPS, 2, 8, G), f32), V((GROUPS, 8, G), f32),
            V((GROUPS,) + two + (8, G), f32),
            V((GROUPS, B, G // GROUPS), f32), V((GROUPS, B // 2, G // GROUPS), f32), V((B // 2, 2 * B), f32),
            V(two + (16, 2 * B), f32), V((2, 2, 2, 16, 2 * B), f32), V((2, 2, 16, 2 * B), f32), V((4, 16, 2 * B), f32),
            DMA((4,)), DMA((4,)), DMA((PARTS, 3)), DMA((PARTS, 3)), DMA((PARTS, 2)), DMA((PARTS, 2)),
            DMA((4,)), DMA((4,))] + [DMA((GROUPS, len(STRIPS), 4))] * 4 + [
            DMA((GROUPS,)), DMA((GROUPS,)), DMA((PARTS, 2)), DMA((PARTS, 2)), DMA((PARTS, 2)), DMA((PARTS, 2)),
            DMA((PARTS,)), DMA((PARTS,)), DMA((3,)), DMA((3,)), DMA((3, PARTS, 4)), DMA((3, PARTS, 4)),
        ],
        1, (mask, kernels, target) + blocks + consts, 59,
    )
    gradient = pl.pallas_call(
        final_kernel,
        out_shape=jax.ShapeDtypeStruct((R, N), f32),
        in_specs=[pl.BlockSpec(memory_space=pltpu.VMEM)] + [any_] * 4,
        out_specs=any_,
        scratch_shapes=slab + [V(t.shape, bf16) for t in parity] + [
            V((2 * groups, B, BLOCK), f32), V((2, R, B), bf16), V((2, R, B), bf16), V((2, 2, R, 256), f32), DMA((2,)), DMA((2,)), DMA((2, 2)),
        ],
        compiler_params=pltpu.CompilerParams(vmem_limit_bytes=48 * 2**20),
    )(total.reshape(B, 2 * B), *blocks, *parity)
    return gradient, resist


def solution(mesh):
    in_specs = (P("space", None), P(None, "kern", "space", None), P("space", None))
    out_specs = (P("space", None), P("space", None))
    S, Q = mesh.shape["space"], mesh.shape["kern"]
    body = functools.partial(fast, S, Q) if (S, Q) == (8, 4) else local
    return jax.shard_map(body, mesh=mesh, in_specs=in_specs, out_specs=out_specs, check_vma=False)
```

```python
import functools

import jax
import jax.numpy as jnp
import ml_dtypes
import numpy as np
from jax import lax
from jax.experimental import pallas as pl
from jax.experimental.pallas import tpu as pltpu
from jax.sharding import PartitionSpec as P

N = 4096
B = 512
G = 1024


steepness = 8.0
threshold = 1.5
highest = lax.Precision.HIGHEST
block_limit = 1024


def phases(left, right, modulus):
    product = left[:, None] * right[None, :] % modulus
    return product.astype(jnp.float32) * (2.0 * jnp.pi / modulus)


def column_table(pixels, frequency, length):
    angle = phases(pixels, frequency, length)
    return jnp.concatenate([jnp.cos(angle), -jnp.sin(angle)], axis=1)


def row_table(pixels, frequency, length):
    angle = phases(pixels, frequency, length)
    return jnp.concatenate([jnp.cos(angle), -jnp.sin(angle)], axis=1) / length


def grid_table(frequency, points):
    angle = phases(frequency, jnp.arange(points, dtype=jnp.int32), points)
    return jnp.concatenate([jnp.cos(angle), jnp.sin(angle)], axis=1)


def forward_columns(mask, frequency):
    rows = mask.shape[0]
    span = min(block_limit, N)
    count = frequency.shape[0]

    def step(index, running):
        start = index * span
        table = column_table(start + jnp.arange(span, dtype=jnp.int32), frequency, N)
        piece = lax.dynamic_slice_in_dim(mask, start, span, 1).astype(jnp.float32)
        return running + lax.dot_general(table, piece, (((0,), (1,)), ((), ())), precision=highest)

    running = lax.fori_loop(0, N // span, step, jnp.zeros((2 * count, rows), jnp.float32))
    return running.reshape(2, count, rows)


def forward_rows(arrived):
    count = arrived.shape[1]
    flat = arrived.reshape(2 * count, N)
    frequency = jnp.arange(B, dtype=jnp.int32) - B // 2
    span = min(block_limit, N)

    def step(index, running):
        start = index * span
        table = row_table(start + jnp.arange(span, dtype=jnp.int32), frequency, N)
        piece = lax.dynamic_slice_in_dim(flat, start, span, 1)
        return running + jnp.dot(piece, table, precision=highest)

    running = lax.fori_loop(0, N // span, step, jnp.zeros((2 * count, 2 * B), jnp.float32))
    real_part = running[:count, :B] - running[count:, B:]
    imag_part = running[:count, B:] + running[count:, :B]
    return jnp.stack([real_part, imag_part])


def adjoint_rows(sum_re, sum_im):
    count = sum_re.shape[0]
    stacked = jnp.concatenate(
        [jnp.concatenate([sum_re, sum_im], axis=1), jnp.concatenate([sum_im, -sum_re], axis=1)],
        axis=0,
    )
    frequency = jnp.arange(B, dtype=jnp.int32) - B // 2
    span = min(block_limit, N)

    def step(index, output):
        start = index * span
        table = row_table(start + jnp.arange(span, dtype=jnp.int32), frequency, N)
        piece = lax.dot_general(stacked, table, (((1,), (1,)), ((), ())), precision=highest)
        return lax.dynamic_update_slice_in_dim(output, piece, start, 1)

    output = lax.fori_loop(0, N // span, step, jnp.zeros((2 * count, N), jnp.float32))
    return output.reshape(2, count, N)


def add_columns(total, spectrum, frequency):
    span = min(block_limit, N)

    def step(index, running):
        start = index * span
        table = column_table(start + jnp.arange(span, dtype=jnp.int32), frequency, N)
        piece = lax.dot_general(spectrum, table, (((0,), (1,)), ((), ())), precision=highest)
        current = lax.dynamic_slice_in_dim(running, start, span, 1)
        return lax.dynamic_update_slice_in_dim(running, current + piece, start, 1)

    return lax.fori_loop(0, N // span, step, total)


def local(mask, kernels, target):
    rows = mask.shape[0]
    kern_count = lax.axis_size("kern")
    space_count = lax.axis_size("space")
    group = lax.axis_index("kern")
    per_space = B // space_count
    per_group = per_space // kern_count
    frequency = jnp.arange(B, dtype=jnp.int32) - B // 2
    subset = (
        per_space * jnp.arange(space_count, dtype=jnp.int32)[:, None]
        + per_group * group
        + jnp.arange(per_group, dtype=jnp.int32)[None, :]
    )
    columns = forward_columns(mask, subset.reshape(-1) - B // 2)
    arrived = lax.all_to_all(columns, "space", split_axis=1, concat_axis=2, tiled=True)
    spectrum = lax.all_gather(forward_rows(arrived), "kern", axis=1, tiled=True)
    kern_swap = jnp.swapaxes(kernels, 1, 2)
    kernel_count = kern_swap.shape[2]
    spec_re = spectrum[0][:, None, :]
    spec_im = spectrum[1][:, None, :]
    prod_re = kern_swap[0] * spec_re - kern_swap[1] * spec_im
    prod_im = kern_swap[0] * spec_im + kern_swap[1] * spec_re
    grid = grid_table(frequency, G)
    lifted = jnp.dot(
        jnp.stack([prod_re, prod_im]).reshape(2 * per_space * kernel_count, B),
        grid,
        precision=highest,
    )
    lifted = lifted.reshape(2, per_space, kernel_count, 2 * G)
    coarse_re = lifted[0, :, :, :G] - lifted[1, :, :, G:]
    coarse_im = lifted[0, :, :, G:] + lifted[1, :, :, :G]
    coarse = jnp.stack([coarse_re, coarse_im], axis=1)
    gathered = lax.all_to_all(coarse, "space", split_axis=3, concat_axis=0, tiled=True)
    grid_rows = gathered.shape[3]
    image = lax.dot_general(
        gathered.reshape(B, 2 * kernel_count * grid_rows),
        grid,
        (((0,), (0,)), ((), ())),
        precision=highest,
    )
    image = image.reshape(2, kernel_count, grid_rows, 2 * G)
    field_re = image[0, :, :, :G] - image[1, :, :, G:]
    field_im = image[0, :, :, G:] + image[1, :, :, :G]
    partial_light = jnp.sum(field_re * field_re + field_im * field_im, axis=0) / (B * B)
    intensity = lax.psum(partial_light, "kern")
    resist = jax.nn.sigmoid(steepness * (intensity - threshold))
    slope = 2.0 * (resist - target.astype(jnp.float32)) * steepness * resist * (1.0 - resist)
    scale = 2.0 * slope / (B * B)
    grad_re = scale * field_re
    grad_im = scale * field_im
    mixed = jnp.stack(
        [
            jnp.concatenate([grad_re, grad_im], axis=-1),
            jnp.concatenate([grad_im, -grad_re], axis=-1),
        ]
    )
    mixed = mixed.reshape(2 * kernel_count * grid_rows, 2 * G)
    backward = lax.dot_general(grid, mixed, (((1,), (1,)), ((), ())), precision=highest)
    backward = backward.reshape(B, 2, kernel_count, grid_rows)
    returned = lax.all_to_all(backward, "space", split_axis=0, concat_axis=3, tiled=True)
    back_re = returned[:, 0]
    back_im = returned[:, 1]
    mixed_two = jnp.stack(
        [
            jnp.concatenate([back_re, back_im], axis=-1),
            jnp.concatenate([back_im, -back_re], axis=-1),
        ]
    )
    mixed_two = mixed_two.reshape(2 * per_space * kernel_count, 2 * G)
    spectral = lax.dot_general(mixed_two, grid, (((1,), (1,)), ((), ())), precision=highest)
    spectral = spectral.reshape(2, per_space, kernel_count, B)
    sum_re = jnp.sum(kern_swap[0] * spectral[0] + kern_swap[1] * spectral[1], axis=1)
    sum_im = jnp.sum(kern_swap[0] * spectral[1] - kern_swap[1] * spectral[0], axis=1)
    empty = jnp.zeros((rows, N), jnp.float32)
    shares = (
        lax.psum_scatter(sum_re, "kern", scatter_dimension=0, tiled=True),
        lax.psum_scatter(sum_im, "kern", scatter_dimension=0, tiled=True),
    )
    delta = adjoint_rows(shares[0], shares[1])
    landed = lax.all_to_all(delta, "space", split_axis=2, concat_axis=1, tiled=True)
    ordering = (
        per_group * jnp.arange(kern_count, dtype=jnp.int32)[:, None, None]
        + per_space * jnp.arange(space_count, dtype=jnp.int32)[None, :, None]
        + jnp.arange(per_group, dtype=jnp.int32)[None, None, :]
    )
    ordered_freq = ordering.reshape(-1) - B // 2
    piece = lax.all_gather(landed, "kern", axis=1, tiled=True)
    width = piece.shape[1]
    gradient = add_columns(empty, piece.reshape(2 * width, rows), ordered_freq)
    return (gradient, resist)


MESH = pl.DeviceIdType.MESH


def split_constant(values):
    high = values.astype(np.float32).astype(ml_dtypes.bfloat16)
    low = (values - high.astype(np.float64)).astype(ml_dtypes.bfloat16)
    return jnp.asarray(high), jnp.asarray(low)


def pixel_tables():
    f = np.arange(B) - B // 2
    angle = (f[:, None] * np.arange(N)) % N * (2 * np.pi / N)
    c, s = np.cos(angle), -np.sin(angle)
    blocks = np.concatenate([c.reshape(B // BLOCK, BLOCK, N), s.reshape(B // BLOCK, BLOCK, N)], 1)
    parity = np.stack([np.concatenate([c[p::2, : N // 2], s[p::2, : N // 2]]) for p in range(2)])
    return split_constant(blocks), split_constant(parity)


def coarse_tables():
    f = np.arange(B) - B // 2
    points = np.arange(G)
    angle = (f[:, None] * points[None, :]) % G * (2 * np.pi / G)
    c, s = np.cos(angle), np.sin(angle)
    order = np.arange(G).reshape(8, 2, 2, GROUPS, 8).transpose(1, 3, 2, 0, 4).reshape(2, GROUPS, G // 2 // GROUPS)
    lift = np.stack([[np.block([[c.T[o], -s.T[o]], [s.T[o], c.T[o]]]) for o in part] for part in order])
    image = np.concatenate([t[:, i : i + w] for i, w in STRIPS for t in (c, s)], 1)
    return split_constant(lift) + split_constant(image)


def halves(value):
    high = value.astype(jnp.bfloat16)
    return high, (value - high.astype(jnp.float32)).astype(jnp.bfloat16)


def dot3(ah, al, bh, bl, dims):
    d = functools.partial(lax.dot_general, dimension_numbers=(dims, ((), ())), preferred_element_type=jnp.float32)
    both, rows = d(jnp.concatenate([ah, al], axis=0), bh), ah.shape[0]
    return both[:rows] + (both[rows:] + d(ah, bl))


NN = ((1,), (0,))
NT = ((1,), (1,))
PARTS = 4
BLOCK = 128
GROUPS = 4
SUM_BEATS = (5, 8, 10, 12)
SPREAD_BEATS = (14, 16, 19, 22)
STRIPS = ((0, 384), (384, 384), (768, 256))
STRIP_ORDERS = ("xylh", "ylxh", "lxyh")
DIMS = "yhlx"
PLANE_ORDERS = ("xy", "yx", "xy", "yx")
SPACE_ORDERS = ("xlh", "lxh", "xlh", "lxh")


def remote(src, dst, send, recv, device):
    return pltpu.make_async_remote_copy(
        src_ref=src, dst_ref=dst, send_sem=send, recv_sem=recv, device_id=device, device_id_type=MESH
    )


def crossed(v):
    return 2 * lax.rem(v, 2) + v // 2


def index(dims, fixed, lanes):
    return tuple(fixed.get(d, slice(None)) for d in dims) + (slice(None), lanes)


def without(dims, gone):
    return "".join(d for d in dims if d not in gone)


class Scatter:
    def __init__(self, me, partner, src, bufs, dims, order, lanes, send, recv, base={}):
        self.me, self.partner, self.refs, self.dims, self.base = me, partner, [src] + list(bufs), dims, base
        self.order, self.lanes, self.send, self.recv = order, lanes, send, recv

    def place(self, t, fixed):
        return index(without(self.dims, self.order[:t]), {**self.base, **fixed}, self.lanes)

    def copy(self, t):
        d = self.order[t]
        return remote(
            self.refs[t].at[self.place(t, {d: 1 - self.me[d]})], self.refs[t + 1].at[self.place(t + 1, {})],
            self.send.at[t], self.recv.at[t], self.partner[d],
        )

    def start(self, t):
        self.copy(t).start()

    def finish(self, t):
        self.copy(t).wait_recv()
        d = self.order[t]
        own = self.refs[t][self.place(t, {d: self.me[d]})]
        there = self.place(t + 1, {})
        self.refs[t + 1][there] = self.refs[t + 1][there] + own

    def drain(self):
        for t in range(len(self.order)):
            self.copy(t).wait_send()


class Gather:
    def __init__(self, me, partner, ref, dims, order, lanes, send, recv, base={}):
        self.me, self.partner, self.ref, self.dims, self.base = me, partner, ref, dims, base
        self.order, self.lanes, self.send, self.recv = order, lanes, send, recv

    def copy(self, t, theirs):
        fixed = {**self.base, **{d: self.me[d] for d in self.order[t:]}}
        if theirs:
            fixed[self.order[t]] = 1 - fixed[self.order[t]]
        view = self.ref.at[index(self.dims, fixed, self.lanes)]
        return remote(view, view, self.send.at[t], self.recv.at[t], self.partner[self.order[t]])

    def start(self, t):
        self.copy(t, False).start()

    def finish(self, t):
        self.copy(t, True).wait_recv()

    def drain(self):
        for t in range(len(self.order)):
            self.copy(t, False).wait_send()


def imaging_kernel(
    mask_hbm, kern_mine, target_hbm, bh_hbm, bl_hbm, lh_hbm, ll_hbm, th_hbm, tl_hbm,
    out_ref, resist_ref,
    lh, ll, th, tl, table_sem, mbuf, fh, fl, load_sem, slabh, slabl, target_ref, slab_sem, columns, part_ref,
    kbuf, p0, p1, p2, spec, ph, pw, cout, cin, ch, cl, field, mh, ml,
    light, l0, l1, l2, l3, slope, grad, gin, acc, sums, s0, s1, s2,
    ks, kr_, ps, pr_, as_, ar, xs, xr, ls, lr, gs, gr, cs, cr, ss, sr_, os_, or_, fs, fr, us, ur, zs, zr,
):
    H, C = G // 2 // GROUPS, B // 2
    sp, kq = lax.axis_index("space"), lax.axis_index("kern")
    z, x = sp // 2, lax.rem(sp, 2)
    y, core = kq // 2, lax.rem(kq, 2)
    me = {"y": y, "h": z // 2, "l": lax.rem(z, 2), "x": x}
    partner = {
        "y": (sp, (1 - y) * 2 + core),
        "x": (z * 2 + 1 - x, kq),
        "l": ((z + 1 - 2 * me["l"]) * 2 + x, kq),
        "h": (lax.rem(z + 2, 4) * 2 + x, kq),
    }
    sibling = (sp, y * 2 + 1 - core)
    lanes = [pl.ds(j * (2 * B // PARTS), 2 * B // PARTS) for j in range(PARTS)]
    strips = [pl.ds(i, w) for i, w in STRIPS]
    span = N // 4

    def loads(i):
        cols = pl.ds(pl.multiple_of(i * span, span), span)
        blk = 2 * core + y
        pairs = [(mask_hbm.at[:, cols], mbuf.at[i]), (bh_hbm.at[blk, :, cols], fh.at[i]), (bl_hbm.at[blk, :, cols], fl.at[i])]
        return [pltpu.make_async_copy(a, b, load_sem.at[i, n]) for n, (a, b) in enumerate(pairs)]

    rows_mine = pl.ds(pl.multiple_of(sp * (N // 8), N // 8), N // 8)
    others = [
        pltpu.make_async_copy(a, b, slab_sem.at[n])
        for n, (a, b) in enumerate(
            [(bh_hbm.at[:, :, rows_mine], slabh), (bl_hbm.at[:, :, rows_mine], slabl), (target_hbm, target_ref)]
        )
    ]
    tables = [
        pltpu.make_async_copy(src, dst, table_sem.at[i])
        for i, (src, dst) in enumerate(zip((lh_hbm, ll_hbm, th_hbm, tl_hbm), (lh, ll, th, tl)))
    ]
    for t in sum([loads(i) for i in range(4)], []) + others:
        t.start()

    far_z = [lax.rem(z + o, 4) for o in range(1, 4)]

    def z_copy(use, j, src, dst, to, slot):
        return remote(src, dst, zs.at[use, j, to], zr.at[use, j, slot], (to * 2 + x, kq))

    def z_block(ref, j, zz):
        return ref.at[index(DIMS, {"y": y, "x": x, "h": zz // 2, "l": lax.rem(zz, 2)}, lanes[j])]

    def z_spread(use, ref, j):
        return [z_copy(use, j, z_block(ref, j, z), z_block(ref, j, z), zz, z) for zz in far_z]

    def z_spread_land(use, ref, j):
        for zz in far_z:
            z_copy(use, j, z_block(ref, j, zz), z_block(ref, j, zz), zz, zz).wait_recv()

    barrier = pltpu.get_barrier_semaphore()
    for device in list(partner.values()) + [sibling, ((3 - z) * 2 + x, kq)]:
        pl.semaphore_signal(barrier, inc=1, device_id=device, device_id_type=MESH)
    half, slot = sp // 4, lax.rem(sp, 4)
    stays = jnp.logical_and(half == core, x == core)
    kinds = [lax.rem(2 * (1 - half) + i, 4) for i in range(4)]
    leaves = [jnp.logical_not(jnp.logical_and(stays, k == z)) for k in kinds]
    comes = [jnp.logical_not(jnp.logical_and(stays, slot == i)) for i in range(4)]
    for i in range(4):
        @pl.when(comes[i])
        def _():
            pl.semaphore_signal(barrier, inc=1, device_id=(core * 4 + i, y * 2 + x), device_id_type=MESH)

    pl.semaphore_wait(barrier, 10 - jnp.where(stays, 1, 0))

    scatter = [
        Scatter(me, partner, part_ref, (p0, p1, p2), "hlx", SPACE_ORDERS[j], lanes[j], ps.at[j], pr_.at[j])
        for j in range(PARTS)
    ]
    gather = [
        Gather(me, partner, spec, DIMS, PLANE_ORDERS[j][::-1], lanes[j], as_.at[j], ar.at[j]) for j in range(PARTS)
    ]
    def kern_copy(i, place):
        k = kinds[i]
        return remote(
            kern_mine.at[:, k], kbuf.at[:, place], ks.at[i], kr_.at[place], (2 * k + core, y * 2 + half)
        )

    def kern_stay():
        return pltpu.make_async_copy(kern_mine.at[:, z], kbuf.at[:, slot], kr_.at[slot])

    def kern_send(i):
        @pl.when(leaves[i])
        def _():
            kern_copy(i, slot).start()

    @pl.when(stays)
    def _():
        kern_stay().start()

    for i in range(4):
        kern_send(i)
    columns[...] = jnp.zeros_like(columns)

    def sweep(i, c):
        for t in loads(i):
            t.wait()
        m = mbuf[i]
        d = functools.partial(lax.dot_general, dimension_numbers=(NT, ((), ())), preferred_element_type=jnp.float32)
        both = d(jnp.concatenate([fh[i], fl[i]], axis=0), m)
        columns[...] += both[: 2 * BLOCK] + both[2 * BLOCK :]
        return c

    lax.fori_loop(0, 4, sweep, 0)
    for t in tables:
        t.start()
    for t in others[:2]:
        t.wait()
    colh, coll = halves(columns[...] * (1.0 / N))

    def band(n, c):
        value = dot3(colh, coll, slabh[n], slabl[n], NT)
        re = value[:BLOCK, :BLOCK] - value[BLOCK:, BLOCK:]
        im = value[:BLOCK, BLOCK:] + value[BLOCK:, :BLOCK]
        at = pl.multiple_of(n * BLOCK, BLOCK)
        part_ref[:, :, :, :, pl.ds(at, BLOCK)] = re.reshape(2, 2, 2, 16, BLOCK)
        part_ref[:, :, :, :, pl.ds(B + at, BLOCK)] = im.reshape(2, 2, 2, 16, BLOCK)
        return c

    lax.fori_loop(0, B // BLOCK, band, 0)
    for one in scatter:
        one.start(0)

    for t in range(3):
        for s in scatter:
            s.finish(t)
            if t < 2:
                s.start(t + 1)
    for j in range(PARTS):
        spec[index(DIMS, me, lanes[j])] = p2[:, lanes[j]]
        for one in z_spread(0, spec, j):
            one.start()
    for j, g in enumerate(gather):
        z_spread_land(0, spec, j)
        g.start(0)
    for t in range(2):
        for g in gather:
            g.finish(t)
            if t < 1:
                g.start(t + 1)
    for i in range(4):
        @pl.when(comes[i])
        def _():
            kern_copy(0, i).wait_recv()

    @pl.when(stays)
    def _():
        kern_stay().wait()

    def product(i, c):
        rows = pl.ds(pl.multiple_of(i * 64, 64), 64)
        kr, ki = kbuf[0, i], kbuf[1, i]
        value = spec[i // 2, lax.rem(i, 2)].reshape(64, 2 * B)
        sr, si = value[:, :B], value[:, B:]
        ph[rows, :B], pw[rows, :B] = halves(kr * sr - ki * si)
        ph[rows, B:], pw[rows, B:] = halves(kr * si + ki * sr)
        return c

    lax.fori_loop(0, 4, product, 0)

    mine = pl.ds(pl.multiple_of(core * C, C), C)
    other = pl.ds(pl.multiple_of((1 - core) * C, C), C)

    def lift(d, g):
        return dot3(lh[d, g], ll[d, g], ph[...], pw[...], NT)

    def cross_copy(g):
        return remote(cout.at[g], cin.at[g], xs.at[g], xr.at[g], sibling)

    def lift_other(g):
        cout[g] = lift(1 - core, g)
        cross_copy(g).start()

    def lift_own(g):
        ch[g, :, mine], cl[g, :, mine] = halves(lift(core, g))

    def cross_land(g):
        cross_copy(g).wait_recv()
        ch[g, :, other], cl[g, :, other] = halves(cin[g])

    def add_light(g):
        return [
            Scatter(
                me, partner, light, (l0, l1, l2, l3), "g" + DIMS, o, strips[i], ls.at[g, i], lr.at[g, i], {"g": g}
            )
            for i, o in enumerate(STRIP_ORDERS)
        ]

    def spread(g):
        return [
            Gather(me, partner, slope, "g" + DIMS, o[::-1], strips[i], gs.at[g, i], gr.at[g, i], {"g": g})
            for i, o in enumerate(STRIP_ORDERS)
        ]

    def image(g, i):
        start, w = STRIPS[i]
        cols = pl.ds(2 * start, 2 * w)
        value = dot3(ch[g], cl[g], th[:, cols], tl[:, cols], NN)
        re = value[:H, :w] - value[H:, w:]
        im = value[:H, w:] + value[H:, :w]
        field[g, :H, strips[i]] = re
        field[g, H:, strips[i]] = im
        light[g, :, :, :, :, :, strips[i]] = (re * re + im * im).reshape(2, 2, 2, 2, 8, w)

    def expose(g, i):
        rows = pl.ds(pl.multiple_of(core * 64 + y * 32 + g * 8, 8), 8)
        intensity = l3[g, :, strips[i]] * (1.0 / (B * B))
        resist = jax.nn.sigmoid(steepness * (intensity - threshold))
        resist_ref[rows, strips[i]] = resist
        goal = target_ref[rows, strips[i]].astype(jnp.float32)
        slope[index("g" + DIMS, {**me, "g": g}, strips[i])] = (
            (4.0 * steepness / (B * B)) * (resist - goal) * resist * (1.0 - resist)
        )

    def back(g):
        for i, (start, w) in enumerate(STRIPS):
            scale = slope[g, :, :, :, :, :, strips[i]].reshape(H, w)
            rh, rl = halves(field[g, :H, strips[i]] * scale)
            ih, il = halves(field[g, H:, strips[i]] * scale)
            one, two = pl.ds(2 * start, w), pl.ds(2 * start + w, w)
            mh[:H, one], mh[:H, two], mh[H:, one], mh[H:, two] = rh, ih, ih, -rh
            ml[:H, one], ml[:H, two], ml[H:, one], ml[H:, two] = rl, il, il, -rl

    def back_rows(g, rows):
        grad[g, rows, :] = dot3(th[rows, :], tl[rows, :], mh[...], ml[...], NT)

    def grad_copy(g):
        return remote(grad.at[g, other], gin.at[g], cs.at[g], cr.at[g], sibling)

    def adjoint(value, d, g):
        dh, dl = halves(value)
        return dot3(dh, dl, lh[d, g], ll[d, g], NN)

    def adjoint_own(g):
        acc[...] = acc[...] + adjoint(grad[g, mine, :], core, g)

    def adjoint_land(g):
        grad_copy(g).wait_recv()
        acc[...] = acc[...] + adjoint(gin[g], 1 - core, g)

    def show(g, i):
        if i == 0:
            lift_own(g)

            @pl.when(g < GROUPS - 1)
            def _():
                lift_other(g + 1)

            cross_land(g)
        image(g, i)
        add_light(g)[i].start(0)

    def add_step(n, g, i):
        s = add_light(g)[i]
        s.finish(n)
        if n < 3:
            s.start(n + 1)
        else:
            expose(g, i)
            spread(g)[i].start(0)

    def spread_step(n, g, i):
        s = spread(g)[i]
        s.finish(n)
        if n < 3:
            s.start(n + 1)

    def back_first(g, i):
        back(g)
        back_rows(g, other)
        grad_copy(g).start()

    def back_second(g, i):
        back_rows(g, mine)

    def back_third(g, i):
        adjoint_own(g)

        @pl.when(g > 0)
        def _():
            adjoint_land(g - 1)

    items = []
    stages = [(0, 1, show)]
    stages += [(SUM_BEATS[n], 2, functools.partial(add_step, n)) for n in range(4)]
    stages += [(SPREAD_BEATS[n], -1 if n == 3 else 0, functools.partial(spread_step, n)) for n in range(4)]
    last = SPREAD_BEATS[3] + 2
    stages += [(last, 0, back_first), (last + 1, 0, back_second), (last + 2, 0, back_third)]
    for beat, rank, body in stages:
        for i in range(len(STRIPS) if beat < last else 1):
            items.append(((beat + i) % len(STRIPS), rank, -beat, (beat + i) // len(STRIPS), i, body))
    items.sort(key=lambda e: e[:3])
    ticks = GROUPS + max(e[3] for e in items)

    def tick(t, c):
        for _, _, _, late, i, body in items:
            g = t - late

            @pl.when(jnp.logical_and(g >= 0, g < GROUPS))
            def _():
                body(g, i)

        return c

    for t in tables + others[2:]:
        t.wait()
    acc[...] = jnp.zeros_like(acc)
    lift_other(0)
    lax.fori_loop(0, ticks, tick, 0)

    def resist_copy(i, rows, device):
        return remote(resist_ref.at[rows], resist_ref.at[rows], us.at[i], ur.at[i], device)

    row_of = lambda c, yy: pl.ds(pl.multiple_of(c * 64 + yy * 32, 32), 32)
    resist_copy(0, row_of(core, y), partner["y"]).start()
    resist_copy(1, row_of(core, y), sibling).start()

    grad_copy(GROUPS - 1).wait_recv()
    gh, gl = halves(gin[GROUPS - 1])
    far = lambda cols: dot3(gh, gl, lh[1 - core, GROUPS - 1, :, cols], ll[1 - core, GROUPS - 1, :, cols], NN)
    add_sums = [
        Scatter(me, partner, sums, (s0, s1), DIMS, PLANE_ORDERS[j], lanes[j], ss.at[j], sr_.at[j])
        for j in range(PARTS)
    ]
    for j in range(2):
        pr = acc[:, lanes[j]] + far(lanes[j])
        pi = acc[:, lanes[j + 2]] + far(lanes[j + 2])
        kr = kbuf[0, :, :, lanes[j]].reshape(C, C)
        ki = kbuf[1, :, :, lanes[j]].reshape(C, C)
        sums[:, :, :, :, :, lanes[j]] = (kr * pr + ki * pi).reshape(2, 2, 2, 2, 16, C)
        add_sums[j].start(0)
        sums[:, :, :, :, :, lanes[j + 2]] = (kr * pi - ki * pr).reshape(2, 2, 2, 2, 16, C)
        add_sums[j + 2].start(0)
    out_mine = out_ref.at[core]
    deliver = [
        Gather(me, partner, out_mine, DIMS, PLANE_ORDERS[j][::-1], lanes[j], os_.at[j], or_.at[j])
        for j in range(PARTS)
    ]

    def part_of(j, zz):
        return s1.at[zz // 2, lax.rem(zz, 2), :, lanes[j]]

    def z_send(j, zz):
        return z_copy(1, j, part_of(j, zz), s2.at[z, :, lanes[j]], zz, z)

    for j, s in enumerate(add_sums):
        s.finish(0)
        s.start(1)
    for j, s in enumerate(add_sums):
        s.finish(1)
        for zz in far_z:
            z_send(j, zz).start()
    for j in range(PARTS):
        value = s1[me["h"], me["l"], :, lanes[j]]
        for zz in far_z:
            z_copy(1, j, part_of(j, zz), s2.at[zz, :, lanes[j]], zz, zz).wait_recv()
            value = value + s2[zz, :, lanes[j]]
        out_ref[(core,) + index(DIMS, me, lanes[j])] = value
        for one in z_spread(2, out_mine, j):
            one.start()

    def final_copy(j, c):
        view = out_ref.at[(c,) + index(DIMS, {}, lanes[j])]
        return remote(view, view, fs.at[j], fr.at[j], sibling)

    for j, g in enumerate(deliver):
        z_spread_land(2, out_mine, j)
        g.start(0)
    for t in range(2):
        for j, g in enumerate(deliver):
            g.finish(t)
            if t < 1:
                g.start(t + 1)
            else:
                final_copy(j, core).start()
    resist_copy(0, row_of(core, 1 - y), partner["y"]).wait_recv()
    resist_copy(2, row_of(core, 1 - y), sibling).start()
    resist_copy(1, row_of(1 - core, y), sibling).wait_recv()
    resist_copy(2, row_of(1 - core, 1 - y), sibling).wait_recv()
    for j in range(PARTS):
        final_copy(j, 1 - core).wait_recv()

    for j in range(PARTS):
        final_copy(j, core).wait_send()
    for j in range(PARTS):
        for one in z_spread(0, spec, j) + [z_send(j, zz) for zz in far_z] + z_spread(2, out_mine, j):
            one.wait_send()
    for group in (scatter, gather, add_sums, deliver):
        for one in group:
            one.drain()

    def drain(g, c):
        for one in add_light(g) + spread(g):
            one.drain()
        cross_copy(g).wait_send()
        grad_copy(g).wait_send()
        return c

    lax.fori_loop(0, GROUPS, drain, 0)
    for i in range(4):
        @pl.when(leaves[i])
        def _():
            kern_copy(i, slot).wait_send()

    resist_copy(0, row_of(core, y), partner["y"]).wait_send()
    resist_copy(1, row_of(core, y), sibling).wait_send()
    resist_copy(2, row_of(core, 1 - y), sibling).wait_send()


def call(kernel, outs, specs, scratch, cid, args, mib):
    vm = pl.BlockSpec(memory_space=pltpu.VMEM)
    return pl.pallas_call(
        kernel,
        out_shape=outs,
        in_specs=specs,
        out_specs=jax.tree.map(lambda _: vm, outs),
        scratch_shapes=scratch,
        compiler_params=pltpu.CompilerParams(
            collective_id=cid, has_side_effects=True, vmem_limit_bytes=mib * 2**20
        ),
    )(*args)


def final_kernel(
    total_hbm, bh_hbm, bl_hbm, eh_hbm, el_hbm, out_hbm,
    total_ref, slabh, slabl, eh, el, split, dh, dl, stage, slab_sem, table_sem, out_sem,
):
    R, W, H = N // 8, 256, N // 2
    sp = lax.axis_index("space")
    rows = pl.ds(pl.multiple_of(sp * R, R), R)
    slabs = [
        pltpu.make_async_copy(src.at[:, :, rows], dst, slab_sem.at[i])
        for i, (src, dst) in enumerate(((bh_hbm, slabh), (bl_hbm, slabl)))
    ]
    tables = [
        pltpu.make_async_copy(src, dst, table_sem.at[i]) for i, (src, dst) in enumerate(((eh_hbm, eh), (el_hbm, el)))
    ]
    arrive = pltpu.make_async_copy(total_hbm, total_ref, slab_sem.at[2])
    for t in [arrive] + slabs:
        t.start()
    arrive.wait()
    for i in range(2 * B // BLOCK):
        split[i] = total_ref[:, pl.ds(i * BLOCK, BLOCK)] * (1.0 / N)
    for t in slabs:
        t.wait()
    for t in tables:
        t.start()
    sh, sl = slabh[...].reshape(2 * B, R), slabl[...].reshape(2 * B, R)
    groups = B // BLOCK
    for p in range(2):
        re = [split[i, pl.ds(p, B // 2, stride=2), :] for i in range(groups)]
        im = [split[groups + i, pl.ds(p, B // 2, stride=2), :] for i in range(groups)]
        re, im = [halves(v) for v in re], [halves(v) for v in im]
        for side in range(2):
            pick = lambda n: jnp.concatenate(
                sum([[re[i][n], im[i][n]] if side == 0 else [im[i][n], -re[i][n]] for i in range(groups)], []), axis=1
            )
            value = dot3(pick(0), pick(1), sh, sl, NN)
            cols = pl.ds(side * (B // 2), B // 2)
            dh[p, :, cols], dl[p, :, cols] = halves(value.T)
    for t in tables:
        t.wait()

    def out_copy(i, half):
        slot = i % 2
        return pltpu.make_async_copy(
            stage.at[slot, half], out_hbm.at[:, pl.ds(half * H + i * W, W)], out_sem.at[slot, half]
        )

    for i in range(H // W):
        cols = pl.ds(i * W, W)
        even = dot3(dh[0], dl[0], eh[0, :, cols], el[0, :, cols], NN)
        odd = dot3(dh[1], dl[1], eh[1, :, cols], el[1, :, cols], NN)
        for half in range(2):
            if i >= 2:
                out_copy(i - 2, half).wait()
            stage[i % 2, half] = even + odd if half == 0 else even - odd
            out_copy(i, half).start()
    for i in range(H // W - 2, H // W):
        for half in range(2):
            out_copy(i, half).wait()


def fast(S, Q, mask, kernels, target):
    f32, bf16 = jnp.float32, jnp.bfloat16
    R, groups = N // S, B // BLOCK
    DMA = pltpu.SemaphoreType.DMA
    any_ = pl.BlockSpec(memory_space=pl.ANY)
    blocks, parity = pixel_tables()
    consts = coarse_tables()
    V = pltpu.VMEM
    two = (2, 2, 2, 2)
    slab = [V((groups, 2 * BLOCK, R), bf16)] * 2
    total, resist = call(
        imaging_kernel,
        (jax.ShapeDtypeStruct((2,) + two + (16, 2 * B), f32), jax.ShapeDtypeStruct((G // S, G), f32)),
        [any_] * 9,
        [V(c.shape, bf16) for c in consts] + [DMA((4,))] + [
            V((4, R, N // 4), bf16), V((4, 2 * BLOCK, N // 4), bf16), V((4, 2 * BLOCK, N // 4), bf16), DMA((4, 3)),
        ] + slab + [V((G // S, G), jnp.int32), DMA((3,)), V((2 * BLOCK, R), f32), V((2, 2, 2, 16, 2 * B), f32)] + [
            V((2, 4, 64, B), f32),
            V((2, 2, 16, 2 * B), f32), V((2, 16, 2 * B), f32), V((16, 2 * B), f32),
            V(two + (16, 2 * B), f32),
            V((B // 2, 2 * B), bf16), V((B // 2, 2 * B), bf16),
            V((4, 256, B // 2), f32), V((4, 256, B // 2), f32),
            V((GROUPS, G // GROUPS, B), bf16), V((GROUPS, G // GROUPS, B), bf16), V((GROUPS, G // GROUPS, G), f32),
            V((G // GROUPS, 2 * G), bf16), V((G // GROUPS, 2 * G), bf16),
            V((GROUPS,) + two + (8, G), f32), V((GROUPS, 2, 2, 2, 8, G), f32), V((GROUPS, 2, 2, 8, G), f32),
            V((GROUPS, 2, 8, G), f32), V((GROUPS, 8, G), f32),
            V((GROUPS,) + two + (8, G), f32),
            V((GROUPS, B, G // GROUPS), f32), V((GROUPS, B // 2, G // GROUPS), f32), V((B // 2, 2 * B), f32),
            V(two + (16, 2 * B), f32), V((2, 2, 2, 16, 2 * B), f32), V((2, 2, 16, 2 * B), f32), V((4, 16, 2 * B), f32),
            DMA((4,)), DMA((4,)), DMA((PARTS, 3)), DMA((PARTS, 3)), DMA((PARTS, 2)), DMA((PARTS, 2)),
            DMA((4,)), DMA((4,))] + [DMA((GROUPS, len(STRIPS), 4))] * 4 + [
            DMA((GROUPS,)), DMA((GROUPS,)), DMA((PARTS, 2)), DMA((PARTS, 2)), DMA((PARTS, 2)), DMA((PARTS, 2)),
            DMA((PARTS,)), DMA((PARTS,)), DMA((3,)), DMA((3,)), DMA((3, PARTS, 4)), DMA((3, PARTS, 4)),
        ],
        1, (mask, kernels, target) + blocks + consts, 59,
    )
    gradient = pl.pallas_call(
        final_kernel,
        out_shape=jax.ShapeDtypeStruct((R, N), f32),
        in_specs=[any_] * 5,
        out_specs=any_,
        scratch_shapes=[V((B, 2 * B), f32)] + slab + [V(t.shape, bf16) for t in parity] + [
            V((2 * groups, B, BLOCK), f32), V((2, R, B), bf16), V((2, R, B), bf16), V((2, 2, R, 256), f32), DMA((3,)), DMA((2,)), DMA((2, 2)),
        ],
        compiler_params=pltpu.CompilerParams(vmem_limit_bytes=59 * 2**20),
    )(total.reshape(B, 2 * B), *blocks, *parity)
    return gradient, resist


def solution(mesh):
    in_specs = (P("space", None), P(None, "kern", "space", None), P("space", None))
    out_specs = (P("space", None), P("space", None))
    S, Q = mesh.shape["space"], mesh.shape["kern"]
    body = functools.partial(fast, S, Q) if (S, Q) == (8, 4) else local
    return jax.shard_map(body, mesh=mesh, in_specs=in_specs, out_specs=out_specs, check_vma=False)
```
